512 devices in a mesh: req: 16 (over x, y_hi, core), mp: 32 (over y_lo, z).
Axes of the slice: x: 4, y: 4 (y_hi: 2, y_lo: 2; y = y_hi * 2 + y_lo), z: 16, core: 2. Of those that a mesh axis runs over, the one named last changes fastest.
Arguments:
- queries: bfloat16 [8192, 8192], P('req', 'mp')
- kv_new: bfloat16 [8192, 32, 256], P('req', 'mp')
- kv_pool: bfloat16 [4096, 16, 32, 256], P('req', None, 'mp')
- ssm_cache: float32 [256, 16, 8192], P('req', None, 'mp'), may hold values from -3 to 3
- mixer_in: bfloat16 [8192, 8192], P('req', 'mp'), may hold values from -3 to 3
- gate_in: bfloat16 [8192, 8192], P('req', 'mp'), may hold values from -2.5 to 2.5
- w_x: bfloat16 [8192, 544], P('mp'), may hold values from -0.0625 to 0.0625
- w_dt: bfloat16 [512, 8192], P(None, 'mp'), may hold values from -0.25 to 0.25
- b_dt: float32 [8192], P('mp'), may hold values from -5 to -1
- a_rate: float32 [16, 8192], P(None, 'mp'), may hold values from 0.05 to 1.5
- d_skip: float32 [8192], P('mp'), may hold values from 0.5 to 1.5
- kept_len: int32 [256], replicated, may hold values from 1 to 256, as said below
- new_len: int32 [256], replicated, may hold values from 1 to 32, as said below
- cache_index: int32 [256], replicated, may hold values from 0 to 255, as said below
- page_table: int32 [256, 16], replicated, may hold values from 0 to 4095, as said below
Outputs:
- attn_out: bfloat16 [8192, 8192], P('req', 'mp')
- mixer_out: bfloat16 [8192, 8192], P('req', 'mp')
- state_out: float32 [256, 16, 8192], P('req', None, 'mp')
The draws below stay inside these ranges and needn't reach their ends.
Inputs may be any that keep to these rules, and one draw needn't show every extreme that they name: `kept_len`: every slot has at least one kept token; some slot has 256. `new_len`: some slot has 32. Every cache entry is named once; the entry of slot s lies on index cache_index[s] // 16 of req; the 16 slots of one index of req take their entries from exactly 8 indices, 2 from each. `page_table`: every page is named once; all pages of slot s lie on the same index of req as its cache entry, that is page // 256 == cache_index[s] // 16.
All inputs are finite; a program needn't handle non-finite values.
Results may differ from the reference program's by a relative error of at most 0.006.
Values may be sent and summed in bfloat16 or wider, within the bound.
No kernel may reach another device: no remote copies, remote signals or barrier semaphores. Data moves between devices by JAX's collectives and lax.ppermute only.
A program may use at most 128 MiB of HBM per device.

```python
import math
import jax
import jax.numpy as jnp
from jax import lax

QH = 64
KVH = 8
HD = 128
NS = 16
R_DT = 512
DI = 8192
BLOCK = 16
REQ_DEV = 16
NEW_MAX = 32
MAXP = 16
KEEP_MAX = 256
POOL_DEV = 256
POOL = 4096
PAIR_MOST = 2
REQUESTS = 256
SLOTS = 8192
P_WIDTH = 544
N_REQ = 16
N_MP = 32


def routing(key):
    key_shift, key_sigma, key_tau, key_local, key_pages = jax.random.split(jax.random.fold_in(key, 101), 5)
    groups = REQ_DEV // PAIR_MOST
    shifts = jax.random.permutation(key_shift, N_REQ)[:groups]
    sigma = jax.random.permutation(key_sigma, N_REQ)
    tau_perm = jax.random.permutation(key_tau, N_REQ)
    slot_ids = jnp.arange(REQUESTS, dtype=jnp.int32)
    rows_of = slot_ids // REQ_DEV
    within = slot_ids % REQ_DEV
    group_of = within // PAIR_MOST
    turn_of = within % PAIR_MOST
    owner = sigma[(tau_perm[rows_of] + shifts[group_of]) % N_REQ]
    local_perm = jax.vmap(lambda one_key: jax.random.permutation(one_key, REQ_DEV))(jax.random.split(key_local, N_REQ))
    entry = owner * REQ_DEV + local_perm[owner, group_of * PAIR_MOST + turn_of]
    page_perm = jax.vmap(lambda one_key: jax.random.permutation(one_key, POOL_DEV))(jax.random.split(key_pages, N_REQ))
    local_entry = entry % REQ_DEV
    columns = local_entry[:, None] * MAXP + jnp.arange(MAXP, dtype=jnp.int32)[None, :]
    pages = owner[:, None] * POOL_DEV + page_perm[owner[:, None], columns]
    return (entry.astype(jnp.int32), pages.astype(jnp.int32))


def draw_cache_index(key, part):
    entry, pages = routing(key)
    return entry


def draw_page_table(key, part):
    entry, pages = routing(key)
    return pages


def draw_kept_len(key, part):
    key = jax.random.fold_in(key, 11)
    key_vals, key_top = jax.random.split(key)
    values = jax.random.randint(key_vals, (REQUESTS,), 1, KEEP_MAX + 1)
    chosen = jax.random.randint(key_top, (), 0, REQUESTS)
    return values.at[chosen].set(KEEP_MAX).astype(jnp.int32)


def draw_new_len(key, part):
    key = jax.random.fold_in(key, 13)
    key_vals, key_top = jax.random.split(key)
    values = jax.random.randint(key_vals, (REQUESTS,), 1, NEW_MAX + 1)
    chosen = jax.random.randint(key_top, (), 0, REQUESTS)
    return values.at[chosen].set(NEW_MAX).astype(jnp.int32)


def draw_queries(key, part):
    key = jax.random.fold_in(key, 21)
    key_vals = jax.random.fold_in(key, 0)
    values = jax.random.normal(key_vals, (SLOTS, QH * HD), jnp.float32)
    return values.astype(jnp.bfloat16)


def draw_kv_new(key, part):
    key = jax.random.fold_in(key, 31)
    values = jax.random.normal(key, (SLOTS, KVH, 2 * HD), jnp.float32)
    return jnp.repeat(values, N_MP // KVH, axis=1).astype(jnp.bfloat16)


def draw_kv_pool(key, part):
    key = jax.random.fold_in(key, 41)
    values = jax.random.normal(key, (POOL, BLOCK, KVH, 2 * HD), jnp.float32)
    return jnp.repeat(values, N_MP // KVH, axis=2).astype(jnp.bfloat16)


def block_levels(rng, dims, cuts, least, top_value):
    def one(position, blocks):
        heights = jax.random.uniform(jax.random.fold_in(jax.random.fold_in(rng, 6), position), (blocks,), jnp.float32, least / len(cuts), top_value / len(cuts))
        return jnp.repeat(jnp.exp(heights), dims[position] // blocks).reshape((-1,) + (1,) * (len(dims) - position - 1))

    level = one(*cuts[0])
    for cut in cuts[1:]:
        level = level * one(*cut)
    return level


def centred(stream_key, extent, deviation, bound, shards=(), held_as=jnp.bfloat16):
    factor_of = block_levels(stream_key, extent, shards, -0.22, 0.18) if shards else 1.0
    array = jax.random.normal(stream_key, extent, jnp.float32) * deviation * factor_of
    return jnp.minimum(jnp.maximum(array, -bound), bound).astype(held_as)


def setup_inputs(seed: int = 0) -> dict:
    seeds = jax.random.split(jax.random.key(seed), 16)
    return {
        "queries": draw_queries(jax.random.fold_in(seeds[15], 71), 0),
        "kv_new": draw_kv_new(jax.random.fold_in(seeds[15], 71), 0),
        "kv_pool": draw_kv_pool(jax.random.fold_in(seeds[15], 71), 0),
        "ssm_cache": centred(seeds[3], (REQUESTS, NS, DI), 0.3, 3.0, ((0, 16), (2, 32)), jnp.float32),
        "mixer_in": centred(seeds[4], (SLOTS, DI), 1.0, 3.0, ((0, 16), (1, 32))),
        "gate_in": centred(seeds[5], (SLOTS, DI), 0.5, 2.5, ((0, 16), (1, 32))),
        "w_x": centred(seeds[6], (DI, P_WIDTH), DI ** -0.5, 0.0625, ((0, 32),)),
        "w_dt": centred(seeds[7], (R_DT, DI), R_DT ** -0.5, 0.25, ((1, 32),)),
        "b_dt": jnp.clip(-5.0 + 4.0 * jax.random.uniform(seeds[8], (DI,), jnp.float32) ** block_levels(seeds[8], (DI,), ((0, 32),), -0.2, 0.2), -5.0, -1.0),
        "a_rate": jnp.clip(jnp.exp(math.log(1.5) - 3.4011974 * jax.random.uniform(seeds[9], (NS, DI), jnp.float32) ** block_levels(seeds[9], (NS, DI), ((1, 32),), -0.2, 0.2)), 0.05, 1.5),
        "d_skip": jnp.clip(0.5 + 1.0 * jax.random.uniform(seeds[10], (DI,), jnp.float32) ** block_levels(seeds[10], (DI,), ((0, 32),), -0.2, 0.2), 0.5, 1.5),
        "kept_len": draw_kept_len(jax.random.fold_in(seeds[15], 71), 0),
        "new_len": draw_new_len(jax.random.fold_in(seeds[15], 71), 0),
        "cache_index": draw_cache_index(jax.random.fold_in(seeds[15], 71), 0),
        "page_table": draw_page_table(jax.random.fold_in(seeds[15], 71), 0),
    }


def selective(delta_t, b_in, c_out, mixer_rows, gate_rows, start_state, new_count, a_rate, d_skip):
    decay = jnp.exp(-delta_t[:, None, :] * a_rate[None, :, :])
    drive = (delta_t * mixer_rows.astype(jnp.float32))[:, None, :] * b_in[:, :, None]

    def combine(earlier, later):
        return (earlier[0] * later[0], later[0] * earlier[1] + later[1])

    cum_decay, cum_drive = lax.associative_scan(combine, (decay, drive), axis=0)
    states = cum_decay * start_state[None, :, :] + cum_drive
    mixed_out = jnp.sum(c_out[:, :, None] * states, axis=1) + d_skip[None, :] * mixer_rows.astype(jnp.float32)
    mixed_out = mixed_out * jax.nn.silu(gate_rows.astype(jnp.float32))
    positions = jnp.arange(delta_t.shape[0], dtype=jnp.int32)
    mixed_out = jnp.where((positions < new_count)[:, None], mixed_out, 0.0).astype(jnp.bfloat16)
    final_state = lax.dynamic_index_in_dim(states, (new_count - 1).astype(jnp.int32), 0, keepdims=False)
    return mixed_out, final_state


def attend(query_rows, fresh, cached, kept, new_count):
    head_copy = jnp.arange(QH, dtype=jnp.int32) // (QH // N_MP)
    key_rows = jnp.concatenate([cached, fresh], 0)[:, head_copy, :].astype(jnp.float32)
    query_heads = query_rows.reshape(NEW_MAX, QH, HD).astype(jnp.float32)
    scores = jnp.einsum('qhd,khd->hqk', query_heads, key_rows[:, :, :HD]) * (HD ** -0.5)
    key_pos = jnp.arange(KEEP_MAX + NEW_MAX, dtype=jnp.int32)
    query_pos = jnp.arange(NEW_MAX, dtype=jnp.int32)
    allowed = jnp.where(key_pos[None, :] < KEEP_MAX, key_pos[None, :] < kept, (key_pos[None, :] - KEEP_MAX) <= query_pos[:, None])
    scores = jnp.where(allowed[None, :, :], scores, -1e30)
    row_max = jnp.max(scores, axis=-1, keepdims=True)
    weights = jnp.exp(scores - row_max)
    total = jnp.sum(weights, axis=-1)
    rounded = lax.optimization_barrier(weights.astype(jnp.bfloat16))
    mixed = jnp.einsum('hqk,khd->qhd', rounded.astype(jnp.float32), key_rows[:, :, HD:])
    mixed = mixed / jnp.transpose(total)[:, :, None]
    mixed = jnp.where((query_pos < new_count)[:, None, None], mixed, 0.0)
    return mixed.reshape(NEW_MAX, QH * HD).astype(jnp.bfloat16)


def reference(queries, kv_new, kv_pool, ssm_cache, mixer_in, gate_in, w_x, w_dt, b_dt, a_rate, d_skip, kept_len, new_len, cache_index, page_table):
    def attend_one(item):
        query_rows, fresh, page_ids, kept, new_count = item
        cached = kv_pool[page_ids].reshape(KEEP_MAX, N_MP, 2 * HD)
        return attend(query_rows, fresh, cached, kept, new_count)

    attn_out = lax.map(attend_one, (queries.reshape(REQUESTS, NEW_MAX, QH * HD), kv_new.reshape(REQUESTS, NEW_MAX, N_MP, 2 * HD), page_table, kept_len, new_len))
    attn_out = attn_out.reshape(SLOTS, QH * HD)
    projected = jnp.dot(mixer_in, w_x, preferred_element_type=jnp.float32)
    low_rank = projected[:, :R_DT].astype(jnp.bfloat16)
    delta_t = jax.nn.softplus(jnp.dot(low_rank, w_dt, preferred_element_type=jnp.float32) + b_dt[None, :])
    b_in = projected[:, R_DT:R_DT + NS]
    c_out = projected[:, R_DT + NS:]
    start_states = ssm_cache[cache_index]

    def scan_one(item):
        return selective(item[0], item[1], item[2], item[3], item[4], item[5], item[6], a_rate, d_skip)

    mixer_out, state_out = lax.map(scan_one, (delta_t.reshape(REQUESTS, NEW_MAX, DI), b_in.reshape(REQUESTS, NEW_MAX, NS), c_out.reshape(REQUESTS, NEW_MAX, NS), mixer_in.reshape(REQUESTS, NEW_MAX, DI), gate_in.reshape(REQUESTS, NEW_MAX, DI), start_states, new_len))
    return attn_out, mixer_out.reshape(SLOTS, DI), state_out
```

```python
import functools

import jax
import jax.numpy as jnp
from jax import lax
from jax.experimental import pallas as pl
from jax.experimental.pallas import tpu as pltpu
from jax.sharding import PartitionSpec as P

BF = jnp.bfloat16
F32 = jnp.float32
LOG2E = 1.4426950408889634

REQ = 16
NEW = 32
HD = 128
PAGES = 16
PAGE = 16
KEEP = PAGES * PAGE
NS = 16
RANK = 512
COLS = 640
CHUNK = 128
SUB = 16
STAT = 64
RET = 72
SEND = 96

VMEM = pl.BlockSpec(memory_space=pltpu.VMEM)
SMEM = pl.BlockSpec(memory_space=pltpu.SMEM)
PARAMS = pltpu.CompilerParams(vmem_limit_bytes=40 * 1024 * 1024)


def pack_kernel(tab, entries, q_ref, cache_ref, out_ref):
    for p in range(REQ):
        for k in range(2):
            slot = tab[k * REQ + p]
            out_ref[p, k * NEW : (k + 1) * NEW, :] = q_ref[
                pl.ds(pl.multiple_of(slot * NEW, NEW), NEW), :
            ]
            entry = entries[p * REQ + tab[(2 + k) * REQ + p]] & (REQ - 1)
            out_ref[p, 2 * NEW + k * NS : 2 * NEW + (k + 1) * NS, :] = cache_ref[entry].astype(BF)


def project_kernel(place, x_ref, w_ref, own_ref, *sent):
    for d in range(4):
        first = pl.multiple_of((place[0] ^ d) * CHUNK, CHUNK)
        rows = x_ref[pl.ds(first, CHUNK), :]
        low = jnp.dot(rows, w_ref[:, :RANK], preferred_element_type=F32)
        rest = jnp.dot(rows, w_ref[:, RANK:], preferred_element_type=F32)
        out = own_ref if d == 0 else sent[d - 1]
        out[:, :RANK] = low.astype(out.dtype)
        pad = jnp.zeros((CHUNK, COLS - RANK - rest.shape[1]), F32)
        out[:, RANK:] = jnp.concatenate([rest, pad], axis=1).astype(out.dtype)


def heads_down(block):
    return jnp.concatenate([block[:, :HD], block[:, HD:]], axis=0)


def cached_kernel(tab, place, table, kept, got_ref, pool_ref, out_ref):
    row = lax.broadcasted_iota(jnp.int32, (2 * NEW, HD), 0)
    lane = lax.broadcasted_iota(jnp.int32, (2 * NEW, HD), 1)
    key = lax.broadcasted_iota(jnp.int32, (2 * NEW, KEEP), 1)
    base = place[1] * (REQ * PAGES)

    def one_peer(p, carry):
        @pl.when(tab[4 * REQ + p] > 0)
        def _():
            stats = []
            for k in range(2):
                slot = p * REQ + tab[(2 + k) * REQ + p]
                pages = [pool_ref[table[slot * PAGES + t] - base] for t in range(PAGES)]
                rows = jnp.concatenate(pages, axis=0)
                q = heads_down(got_ref[p, k * NEW : (k + 1) * NEW, :])
                s = lax.dot_general(
                    q, rows[:, :HD], (((1,), (1,)), ((), ())), preferred_element_type=F32
                ) * (HD**-0.5)
                s = jnp.where(key < kept[slot], s, -1e30)
                top = jnp.max(s, axis=1, keepdims=True)
                w = jnp.exp(s - top)
                total = jnp.sum(w, axis=1, keepdims=True)
                o = jnp.dot(w.astype(BF), rows[:, HD:], preferred_element_type=F32) / total
                out_ref[p, k * NEW : (k + 1) * NEW, :] = jnp.concatenate(
                    [o[:NEW], o[NEW:]], axis=1
                ).astype(BF)
                lse = top + jnp.log(total)
                stats.append(jnp.sum(jnp.where(row == lane, lse, 0.0), axis=0, keepdims=True))
            flat = jnp.concatenate(stats, axis=0)
            hi = flat.astype(BF).astype(F32)
            mid = (flat - hi).astype(BF).astype(F32)
            low = flat - hi - mid
            none = jnp.zeros((6, HD), F32)
            left = jnp.concatenate([hi, low, none[:4]], axis=0)
            right = jnp.concatenate([mid, none], axis=0)
            out_ref[p, STAT:RET, :] = jnp.concatenate([left, right], axis=1).astype(BF)

        return carry

    lax.fori_loop(0, REQ, one_peer, 0)


def combine_kernel(tab, fresh_len, q_ref, kv_ref, got_ref, out_ref):
    row = lax.broadcasted_iota(jnp.int32, (2 * NEW, HD), 0)
    lane = lax.broadcasted_iota(jnp.int32, (2 * NEW, HD), 1)
    query = lax.broadcasted_iota(jnp.int32, (2 * NEW, NEW), 0) & (NEW - 1)
    key = lax.broadcasted_iota(jnp.int32, (2 * NEW, NEW), 1)
    place = lax.broadcasted_iota(jnp.int32, (NEW, 2 * HD), 0)

    def one_slot(i, carry):
        first = pl.multiple_of(i * NEW, NEW)
        owner = tab[5 * REQ + i]
        second = (tab[REQ + owner] == i).astype(jnp.int32)
        q = heads_down(q_ref[pl.ds(first, NEW), :])
        rows = kv_ref[pl.ds(first, NEW), :]
        s = lax.dot_general(
            q, rows[:, :HD], (((1,), (1,)), ((), ())), preferred_element_type=F32
        ) * (HD**-0.5)
        s = jnp.where(key <= query, s, -1e30)
        top = jnp.max(s, axis=1, keepdims=True)
        w = jnp.exp(s - top)
        total = jnp.sum(w, axis=1, keepdims=True)
        o = jnp.dot(w.astype(BF), rows[:, HD:], preferred_element_type=F32)
        old = heads_down(
            got_ref[owner, pl.ds(pl.multiple_of(second * NEW, NEW), NEW), :]
        ).astype(F32)
        stats = got_ref[owner, STAT:RET, :].astype(F32)
        exact = stats[0:2, :HD] + stats[0:2, HD:] + stats[2:4, :HD]
        flat = jnp.where(second > 0, exact[1:2], exact[0:1])
        lse = jnp.sum(jnp.where(row == lane, flat, 0.0), axis=1, keepdims=True)
        most = jnp.maximum(lse, top)
        share_old = jnp.exp(lse - most)
        share = jnp.exp(top - most)
        o = (old * share_old + o * share) / (share_old + total * share)
        o = jnp.concatenate([o[:NEW], o[NEW:]], axis=1)
        out_ref[pl.ds(first, NEW), :] = jnp.where(place < fresh_len[i], o, 0.0).astype(BF)
        return carry

    lax.fori_loop(0, REQ, one_slot, 0, unroll=2)


def scan_kernel(
    tab, place, fresh_len, p0, p1, p2, p3, wdt_ref, b_ref, a_ref, d_ref, x_ref, g_ref, got_ref,
    out_ref, state_ref, dt_s, u_s, bc_s, y_s, a_s, h_s,
):
    channels = x_ref.shape[1]
    halves = [slice(c * HD, (c + 1) * HD) for c in range(channels // HD)]
    step = lax.broadcasted_iota(jnp.int32, (NEW, channels), 0)
    for d, part in enumerate((p0, p1, p2, p3)):
        member = place[0] ^ d
        first = pl.multiple_of(member * CHUNK, CHUNK)
        pre = jnp.dot(part[:, :RANK], wdt_ref[...], preferred_element_type=F32) + b_ref[...]
        dt = jnp.maximum(pre, 0.0) + jnp.log1p(jnp.exp(-jnp.abs(pre)))
        bc_s[pl.ds(first, CHUNK), :] = part[:, RANK:].astype(F32)
        for j in range(CHUNK // NEW):
            here = pl.multiple_of(first + j * NEW, NEW)
            live = step < fresh_len[member * (CHUNK // NEW) + j]
            masked = jnp.where(live, dt[j * NEW : (j + 1) * NEW], 0.0)
            drive = masked * x_ref[pl.ds(here, NEW), :].astype(F32)
            for c, half in enumerate(halves):
                dt_s[c, pl.ds(here, NEW), :] = masked[:, half]
                u_s[c, pl.ds(here, NEW), :] = drive[:, half]
    for i in range(REQ):
        owner = tab[5 * REQ + i]
        second = (tab[REQ + owner] == i).astype(jnp.int32)
        start = pl.multiple_of(2 * NEW + second * NS, NS)
        state = got_ref[owner, pl.ds(start, NS), :].astype(F32)
        for c, half in enumerate(halves):
            h_s[c, i * NS : (i + 1) * NS, :] = state[:, half]
    for n in range(NS):
        a_s[n * 8 : (n + 1) * 8, :] = jnp.broadcast_to(a_ref[n : n + 1, :] * (-LOG2E), (8, channels))
    for g in range(2):
        begin = g * 8 * NS
        h0 = tuple(
            tuple(h_s[c, pl.ds(begin + n, 8, stride=NS), :] for c in range(len(halves)))
            for n in range(NS)
        )

        def one_step(i, hs):
            rows = pl.ds(g * 8 * NEW + i, 8, stride=NEW)
            dt = [dt_s[c, rows, :] for c in range(len(halves))]
            u = [u_s[c, rows, :] for c in range(len(halves))]
            bc = bc_s[rows, :]
            y = [0.0] * len(halves)
            new = []
            for n in range(NS):
                b_in = jnp.broadcast_to(bc[:, n : n + 1], (8, HD))
                c_out = jnp.broadcast_to(bc[:, NS + n : NS + n + 1], (8, HD))
                pair = []
                for c, half in enumerate(halves):
                    decay = jnp.exp2(dt[c] * a_s[n * 8 : (n + 1) * 8, half])
                    h = decay * hs[n][c] + u[c] * b_in
                    y[c] = y[c] + h * c_out
                    pair.append(h)
                new.append(tuple(pair))
            for c in range(len(halves)):
                y_s[c, rows, :] = y[c]
            return tuple(new)

        hs = lax.fori_loop(0, NEW, one_step, h0)
        for n in range(NS):
            for c in range(len(halves)):
                h_s[c, pl.ds(begin + n, 8, stride=NS), :] = hs[n][c]
    for c, half in enumerate(halves):
        state_ref[:, half] = h_s[c]
    for i in range(REQ):
        rows = slice(i * NEW, (i + 1) * NEW)
        for c, half in enumerate(halves):
            gate = g_ref[rows, half].astype(F32)
            y = y_s[c, rows, :] + d_ref[:, half] * x_ref[rows, half].astype(F32)
            y = y * (gate * jax.nn.sigmoid(gate))
            out_ref[rows, half] = jnp.where(step[:, half] < fresh_len[i], y, 0.0).astype(BF)


def on_device(
    queries, kv_new, kv_pool, ssm_cache, mixer_in, gate_in, w_x, w_dt, b_dt, a_rate, d_skip,
    kept_len, new_len, cache_index, page_table,
):
    rows, channels = mixer_in.shape
    me = lax.axis_index("req")
    at = lax.axis_index("mp")
    zs = lax.axis_size("mp") // 2
    member = (at // zs) * 2 + (at & 1)
    place = jnp.stack([member, me]).astype(jnp.int32)

    owners = cache_index.reshape(REQ, REQ) // REQ
    mine = lax.dynamic_slice_in_dim(owners, me, 1, 0)
    ids = jnp.arange(REQ, dtype=jnp.int32)

    def ends(match):
        first = jnp.min(jnp.where(match, ids[None, :], REQ), axis=1)
        last = jnp.max(jnp.where(match, ids[None, :], -1), axis=1)
        return jnp.minimum(first, REQ - 1), jnp.maximum(last, 0), last >= 0

    q_first, q_last, _ = ends(mine == ids[:, None])
    s_first, s_last, active = ends(owners == me)
    tab = jnp.concatenate([q_first, q_last, s_first, s_last, active.astype(jnp.int32), mine[0]])
    fresh_len = lax.dynamic_slice_in_dim(new_len, me * REQ, REQ, 0)

    packed = pl.pallas_call(
        pack_kernel,
        out_shape=jax.ShapeDtypeStruct((REQ, SEND, channels), BF),
        in_specs=[SMEM, SMEM, VMEM, VMEM],
        out_specs=VMEM,
        compiler_params=PARAMS,
        name="pack",
    )(tab, cache_index, queries, ssm_cache)
    got = lax.all_to_all(packed, "req", 0, 0, tiled=True)

    chunk = jax.ShapeDtypeStruct((CHUNK, COLS), BF)
    own, *sent = pl.pallas_call(
        project_kernel,
        out_shape=[jax.ShapeDtypeStruct((CHUNK, COLS), F32), chunk, chunk, chunk],
        in_specs=[SMEM, VMEM, VMEM],
        out_specs=[VMEM] * 4,
        compiler_params=PARAMS,
        name="project",
    )(place, mixer_in, w_x)

    def swap(array, d):
        pairs = []
        for i in range(2 * zs):
            y, z = i // zs, i % zs
            pairs.append((i, (y ^ (d >> 1)) * zs + (z ^ (d & 1))))
        return lax.ppermute(array, "mp", pairs)

    groups = [[y * zs + 2 * k + b for k in range(zs // 2)] for y in range(2) for b in range(2)]
    for d in (1, 2, 3):
        own = own + swap(sent[d - 1], d).astype(F32)
    parts = lax.all_to_all(
        own.astype(BF).reshape(-1, SUB, COLS), "mp", 0, 0, tiled=True, axis_index_groups=groups
    )
    summed = jnp.sum(parts.astype(F32), axis=0, keepdims=True).astype(BF)
    whole = lax.all_to_all(
        jnp.broadcast_to(summed, parts.shape), "mp", 0, 0, tiled=True, axis_index_groups=groups
    ).reshape(CHUNK, COLS)
    others = [swap(whole, d) for d in (1, 2, 3)]

    partial = pl.pallas_call(
        cached_kernel,
        out_shape=jax.ShapeDtypeStruct((REQ, RET, channels), BF),
        in_specs=[SMEM, SMEM, SMEM, SMEM, VMEM, VMEM],
        out_specs=VMEM,
        compiler_params=PARAMS,
        name="cached",
    )(tab, place, page_table.reshape(-1), kept_len, got, kv_pool.reshape(-1, PAGE, channels))
    back = lax.all_to_all(partial, "req", 0, 0, tiled=True)

    mixer_out, state_out = pl.pallas_call(
        scan_kernel,
        out_shape=[
            jax.ShapeDtypeStruct((rows, channels), BF),
            jax.ShapeDtypeStruct((REQ * NS, channels), F32),
        ],
        in_specs=[SMEM] * 3 + [VMEM] * 11,
        out_specs=[VMEM] * 2,
        scratch_shapes=[
            pltpu.VMEM((channels // HD, rows, HD), F32),
            pltpu.VMEM((channels // HD, rows, HD), F32),
            pltpu.VMEM((rows, COLS - RANK), F32),
            pltpu.VMEM((channels // HD, rows, HD), F32),
            pltpu.VMEM((NS * 8, channels), F32),
            pltpu.VMEM((channels // HD, REQ * NS, HD), F32),
        ],
        compiler_params=PARAMS,
        name="scan",
    )(
        tab, place, fresh_len, whole, *others, w_dt, b_dt.reshape(1, -1), a_rate,
        d_skip.reshape(1, -1), mixer_in, gate_in, got,
    )
    attn_out = pl.pallas_call(
        combine_kernel,
        out_shape=jax.ShapeDtypeStruct((rows, channels), BF),
        in_specs=[SMEM, SMEM, VMEM, VMEM, VMEM],
        out_specs=VMEM,
        compiler_params=PARAMS,
        name="combine",
    )(tab, fresh_len, queries, kv_new.reshape(rows, channels), back)
    return attn_out, mixer_out, state_out.reshape(REQ, NS, channels)


def solution(mesh):
    placed = (
        P("req", "mp"),
        P("req", "mp", None),
        P("req", None, "mp", None),
        P("req", None, "mp"),
        P("req", "mp"),
        P("req", "mp"),
        P("mp", None),
        P(None, "mp"),
        P("mp"),
        P(None, "mp"),
        P("mp"),
        P(),
        P(),
        P(),
        P(),
    )
    return jax.shard_map(
        on_device,
        mesh=mesh,
        in_specs=placed,
        out_specs=(P("req", "mp"), P("req", "mp"), P("req", None, "mp")),
        check_vma=False,
    )
```

```python
import functools

import jax
import jax.numpy as jnp
from jax import lax
from jax.experimental import pallas as pl
from jax.experimental.pallas import tpu as pltpu
from jax.sharding import PartitionSpec as P

BF = jnp.bfloat16
F32 = jnp.float32
LOG2E = 1.4426950408889634

REQ = 16
NEW = 32
HD = 128
PAGES = 16
PAGE = 16
KEEP = PAGES * PAGE
NS = 16
RANK = 512
COLS = 640
CHUNK = 128
BC = 2 * NS
SUB = 16
STAT = 64
RET = 72
SEND = 96

VMEM = pl.BlockSpec(memory_space=pltpu.VMEM)
ANY = pl.BlockSpec(memory_space=pl.ANY)
HBM = pl.BlockSpec(memory_space=pltpu.HBM)
SMEM = pl.BlockSpec(memory_space=pltpu.SMEM)
PARAMS = pltpu.CompilerParams(vmem_limit_bytes=60 * 1024 * 1024)


def tail_of(rest):
    lane = lax.broadcasted_iota(jnp.int32, rest.shape, 1)
    high = rest.astype(BF).astype(F32)
    low = pltpu.roll(rest - high, BC, 1)
    return jnp.where(lane < BC, high, jnp.where(lane < 2 * BC, low, 0.0))


def whole_tail(tail):
    return tail + pltpu.roll(tail, tail.shape[1] - BC, 1)


def fetch(pairs, sems):
    copies = [pltpu.make_async_copy(a, b, sems.at[i]) for i, (a, b) in enumerate(pairs)]
    for copy in copies:
        copy.start()
    return copies


def pack_kernel(tab, entries_hbm, q_hbm, cache_hbm, out_ref, entries, q_ref, cache_ref, sems):
    copies = fetch([(entries_hbm, entries), (q_hbm, q_ref), (cache_hbm, cache_ref)], sems)
    for copy in copies:
        copy.wait()
    for p in range(REQ):
        for k in range(2):
            slot = tab[k * REQ + p]
            out_ref[p, k * NEW : (k + 1) * NEW, :] = q_ref[
                pl.ds(pl.multiple_of(slot * NEW, NEW), NEW), :
            ]
            entry = entries[p * REQ + tab[(2 + k) * REQ + p]] & (REQ - 1)
            out_ref[p, 2 * NEW + k * NS : 2 * NEW + (k + 1) * NS, :] = cache_ref[entry].astype(BF)


def project_kernel(place, x_ref, w_ref, after, own_ref, *sent):
    for d in range(4):
        first = pl.multiple_of((place[0] ^ d) * CHUNK, CHUNK)
        rows = x_ref[pl.ds(first, CHUNK), :]
        low = jnp.dot(rows, w_ref[:, :RANK], preferred_element_type=F32)
        rest = jnp.dot(rows, w_ref[:, RANK:], preferred_element_type=F32)
        rest = jnp.concatenate([rest, jnp.zeros((CHUNK, COLS - RANK - BC), F32)], axis=1)
        if d == 0:
            own_ref[:, :RANK] = low
            own_ref[:, RANK:] = rest
        else:
            sent[d - 1][:, :RANK] = low.astype(BF)
            sent[d - 1][:, RANK:] = tail_of(rest).astype(BF)


def add_four_kernel(own_hbm, h1, h2, h3, after, out_ref, own_ref, r1, r2, r3, sems):
    for copy in fetch([(own_hbm, own_ref), (h1, r1), (h2, r2), (h3, r3)], sems):
        copy.wait()
    low = own_ref[:, :RANK]
    tail = jnp.zeros((CHUNK, COLS - RANK), F32)
    for r in (r1, r2, r3):
        low = low + r[:, :RANK].astype(F32)
        tail = tail + r[:, RANK:].astype(F32)
    rest = own_ref[:, RANK:] + whole_tail(tail)
    low = low.astype(BF)
    tail = tail_of(rest).astype(BF)
    for k in range(CHUNK // SUB):
        out_ref[k, :, :RANK] = low[k * SUB : (k + 1) * SUB]
        out_ref[k, :, RANK:] = tail[k * SUB : (k + 1) * SUB]


def add_eight_kernel(parts, after, out_ref):
    total = parts[0].astype(F32)
    for k in range(1, CHUNK // SUB):
        total = total + parts[k].astype(F32)
    low = total[:, :RANK].astype(BF)
    tail = tail_of(whole_tail(total[:, RANK:])).astype(BF)
    for k in range(CHUNK // SUB):
        out_ref[k, :, :RANK] = low
        out_ref[k, :, RANK:] = tail


def gate_kernel(partial, a, b, c, out):
    pass


def heads_down(block):
    return jnp.concatenate([block[:, :HD], block[:, HD:]], axis=0)


def cached_kernel(tab, place, table, kept, got_ref, pool_ref, out_ref):
    row = lax.broadcasted_iota(jnp.int32, (2 * NEW, HD), 0)
    lane = lax.broadcasted_iota(jnp.int32, (2 * NEW, HD), 1)
    key = lax.broadcasted_iota(jnp.int32, (2 * NEW, KEEP), 1)
    base = place[1] * (REQ * PAGES)

    def one_peer(p, carry):
        @pl.when(tab[4 * REQ + p] > 0)
        def _():
            stats = []
            for k in range(2):
                slot = p * REQ + tab[(2 + k) * REQ + p]
                pages = [pool_ref[table[t * REQ * REQ + slot] - base] for t in range(PAGES)]
                rows = jnp.concatenate(pages, axis=0)
                q = heads_down(got_ref[p, k * NEW : (k + 1) * NEW, :])
                s = lax.dot_general(
                    q, rows[:, :HD], (((1,), (1,)), ((), ())), preferred_element_type=F32
                ) * (HD**-0.5)
                s = jnp.where(key < kept[slot], s, -1e30)
                top = jnp.max(s, axis=1, keepdims=True)
                w = jnp.exp(s - top)
                total = jnp.sum(w, axis=1, keepdims=True)
                o = jnp.dot(w.astype(BF), rows[:, HD:], preferred_element_type=F32) / total
                out_ref[p, k * NEW : (k + 1) * NEW, :] = jnp.concatenate(
                    [o[:NEW], o[NEW:]], axis=1
                ).astype(BF)
                lse = top + jnp.log(total)
                stats.append(jnp.sum(jnp.where(row == lane, lse, 0.0), axis=0, keepdims=True))
            flat = jnp.concatenate(stats, axis=0)
            hi = flat.astype(BF).astype(F32)
            mid = (flat - hi).astype(BF).astype(F32)
            low = flat - hi - mid
            none = jnp.zeros((6, HD), F32)
            left = jnp.concatenate([hi, low, none[:4]], axis=0)
            right = jnp.concatenate([mid, none], axis=0)
            out_ref[p, STAT:RET, :] = jnp.concatenate([left, right], axis=1).astype(BF)

        return carry

    lax.fori_loop(0, REQ, one_peer, 0)


def fresh_kernel(q_ref, kv_ref, out_ref, stat_ref):
    row = lax.broadcasted_iota(jnp.int32, (2 * NEW, HD), 0)
    lane = lax.broadcasted_iota(jnp.int32, (2 * NEW, HD), 1)
    query = lax.broadcasted_iota(jnp.int32, (2 * NEW, NEW), 0) & (NEW - 1)
    key = lax.broadcasted_iota(jnp.int32, (2 * NEW, NEW), 1)

    def one_slot(i, carry):
        first = pl.multiple_of(i * NEW, NEW)
        q = heads_down(q_ref[pl.ds(first, NEW), :])
        rows = kv_ref[pl.ds(first, NEW), :]
        s = lax.dot_general(
            q, rows[:, :HD], (((1,), (1,)), ((), ())), preferred_element_type=F32
        ) * (HD**-0.5)
        s = jnp.where(key <= query, s, -1e30)
        top = jnp.max(s, axis=1, keepdims=True)
        w = jnp.exp(s - top)
        total = jnp.sum(w, axis=1, keepdims=True)
        out_ref[i] = jnp.dot(w.astype(BF), rows[:, HD:], preferred_element_type=F32) / total
        lse = top + jnp.log(total)
        flat = jnp.sum(jnp.where(row == lane, lse, 0.0), axis=0, keepdims=True)
        stat_ref[i] = jnp.broadcast_to(flat, (8, HD))
        return carry

    lax.fori_loop(0, REQ, one_slot, 0, unroll=4)


def combine_kernel(place, tab, entries, fresh_len, part_ref, stat_ref, got_ref, after, out_ref):
    row = lax.broadcasted_iota(jnp.int32, (2 * NEW, HD), 0)
    lane = lax.broadcasted_iota(jnp.int32, (2 * NEW, HD), 1)
    spot = lax.broadcasted_iota(jnp.int32, (NEW, 2 * HD), 0)

    def one_slot(i, carry):
        first = pl.multiple_of(i * NEW, NEW)
        owner = entries[place[1] * REQ + i] // REQ
        second = (tab[REQ + owner] == i).astype(jnp.int32)
        old = heads_down(
            got_ref[owner, pl.ds(pl.multiple_of(second * NEW, NEW), NEW), :]
        ).astype(F32)
        stats = got_ref[owner, STAT:RET, :].astype(F32)
        exact = stats[0:2, :HD] + stats[0:2, HD:] + stats[2:4, :HD]
        lse_old = jnp.where(second > 0, exact[1:2], exact[0:1])
        lse = stat_ref[i, 0:1, :]
        most = jnp.maximum(lse_old, lse)
        weight_old = jnp.exp(lse_old - most)
        weight = jnp.exp(lse - most)
        share_old = weight_old / (weight_old + weight)
        share_old = jnp.sum(jnp.where(row == lane, share_old, 0.0), axis=1, keepdims=True)
        share = weight / (weight_old + weight)
        share = jnp.sum(jnp.where(row == lane, share, 0.0), axis=1, keepdims=True)
        o = old * share_old + part_ref[i] * share
        o = jnp.concatenate([o[:NEW], o[NEW:]], axis=1)
        live = spot < fresh_len[place[1] * REQ + i]
        out_ref[pl.ds(first, NEW), :] = jnp.where(live, o, 0.0).astype(BF)
        return carry

    lax.fori_loop(0, REQ, one_slot, 0, unroll=4)


def scan_kernel(
    place, tab, entries, fresh_len, p0, p1, p2, p3, wdt_hbm, b_ref, a_ref, d_ref, x_hbm, g_hbm, got_hbm,
    out_ref, state_ref, done_ref, dt_s, u_s, bc_s, y_s, a_s, h_s, wdt_ref, x_ref, g_ref, got_ref, sems,
):
    copies = fetch(
        [(wdt_hbm, wdt_ref), (x_hbm, x_ref), (got_hbm, got_ref), (g_hbm, g_ref)], sems
    )
    done_ref[...] = jnp.zeros(done_ref.shape, F32)
    channels = x_ref.shape[1]
    halves = [slice(c * HD, (c + 1) * HD) for c in range(channels // HD)]
    step = lax.broadcasted_iota(jnp.int32, (NEW, channels), 0)
    for n in range(NS):
        a_s[n * 8 : (n + 1) * 8, :] = jnp.broadcast_to(a_ref[n : n + 1, :] * (-LOG2E), (8, channels))
    copies[0].wait()
    copies[1].wait()
    for d, part in enumerate((p0, p1, p2, p3)):
        member = place[0] ^ d
        first = pl.multiple_of(member * CHUNK, CHUNK)
        pre = jnp.dot(part[:, :RANK], wdt_ref[...], preferred_element_type=F32) + b_ref[...]
        dt = jnp.maximum(pre, 0.0) + jnp.log1p(jnp.exp(-jnp.abs(pre)))
        bc_s[pl.ds(first, CHUNK), :] = whole_tail(part[:, RANK:].astype(F32))
        for j in range(CHUNK // NEW):
            here = pl.multiple_of(first + j * NEW, NEW)
            live = step < fresh_len[place[1] * REQ + member * (CHUNK // NEW) + j]
            masked = jnp.where(live, dt[j * NEW : (j + 1) * NEW], 0.0)
            drive = masked * x_ref[pl.ds(here, NEW), :].astype(F32)
            for c, half in enumerate(halves):
                dt_s[c, pl.ds(here, NEW), :] = masked[:, half]
                u_s[c, pl.ds(here, NEW), :] = drive[:, half]
    copies[2].wait()
    for i in range(REQ):
        owner = entries[place[1] * REQ + i] // REQ
        second = (tab[REQ + owner] == i).astype(jnp.int32)
        start = pl.multiple_of(2 * NEW + second * NS, NS)
        state = got_ref[owner, pl.ds(start, NS), :].astype(F32)
        for c, half in enumerate(halves):
            h_s[c, i * NS : (i + 1) * NS, :] = state[:, half]
    for g in range(2):
        begin = g * 8 * NS
        h0 = tuple(
            tuple(h_s[c, pl.ds(begin + n, 8, stride=NS), :] for c in range(len(halves)))
            for n in range(NS)
        )

        def one_step(i, hs):
            rows = pl.ds(g * 8 * NEW + i, 8, stride=NEW)
            dt = [dt_s[c, rows, :] for c in range(len(halves))]
            u = [u_s[c, rows, :] for c in range(len(halves))]
            bc = bc_s[rows, :]
            y = [0.0] * len(halves)
            new = []
            for n in range(NS):
                b_in = jnp.broadcast_to(bc[:, n : n + 1], (8, HD))
                c_out = jnp.broadcast_to(bc[:, NS + n : NS + n + 1], (8, HD))
                pair = []
                for c, half in enumerate(halves):
                    decay = jnp.exp2(dt[c] * a_s[n * 8 : (n + 1) * 8, half])
                    h = decay * hs[n][c] + u[c] * b_in
                    y[c] = y[c] + h * c_out
                    pair.append(h)
                new.append(tuple(pair))
            for c in range(len(halves)):
                y_s[c, rows, :] = y[c]
            return tuple(new)

        hs = lax.fori_loop(0, NEW, one_step, h0, unroll=8)
        for n in range(NS):
            for c in range(len(halves)):
                h_s[c, pl.ds(begin + n, 8, stride=NS), :] = hs[n][c]
    for c, half in enumerate(halves):
        state_ref[:, half] = h_s[c]
    copies[3].wait()
    for i in range(REQ):
        rows = slice(i * NEW, (i + 1) * NEW)
        for c, half in enumerate(halves):
            gate = g_ref[rows, half].astype(F32)
            y = y_s[c, rows, :] + d_ref[:, half] * x_ref[rows, half].astype(F32)
            y = y * (gate * jax.nn.sigmoid(gate))
            out_ref[rows, half] = jnp.where(step[:, half] < fresh_len[place[1] * REQ + i], y, 0.0).astype(BF)


def on_device(
    queries, kv_new, kv_pool, ssm_cache, mixer_in, gate_in, w_x, w_dt, b_dt, a_rate, d_skip,
    kept_len, new_len, cache_index, page_table,
):
    rows, channels = mixer_in.shape
    me = lax.axis_index("req")
    at = lax.axis_index("mp")
    zs = lax.axis_size("mp") // 2
    member = (at // zs) * 2 + (at & 1)
    place = jnp.stack([member, me]).astype(jnp.int32)

    slots = jnp.arange(REQ * REQ, dtype=jnp.int32)[None, :]
    peers = jnp.arange(REQ, dtype=jnp.int32)[:, None]
    owners = (cache_index // REQ)[None, :]

    def ends(match):
        first = jnp.min(jnp.where(match, slots & (REQ - 1), REQ - 1), axis=1)
        last = jnp.max(jnp.where(match, slots & (REQ - 1), -1), axis=1)
        return first, jnp.maximum(last, 0), (last >= 0).astype(jnp.int32)

    q_first, q_last, _ = ends((owners == peers) & (slots // REQ == me))
    s_first, s_last, active = ends((owners == me) & (slots // REQ == peers))
    tab = jnp.concatenate([q_first, q_last, s_first, s_last, active])

    packed = pl.pallas_call(
        pack_kernel,
        out_shape=jax.ShapeDtypeStruct((REQ, SEND, channels), BF),
        in_specs=[SMEM, HBM, HBM, HBM],
        out_specs=VMEM,
        scratch_shapes=[
            pltpu.SMEM(cache_index.shape, jnp.int32),
            pltpu.VMEM(queries.shape, BF),
            pltpu.VMEM(ssm_cache.shape, F32),
            pltpu.SemaphoreType.DMA((3,)),
        ],
        compiler_params=PARAMS,
        name="pack",
    )(tab, cache_index, queries, ssm_cache)
    got = lax.all_to_all(packed, "req", 0, 0, tiled=True)

    chunk = jax.ShapeDtypeStruct((CHUNK, COLS), BF)
    own, *sent = pl.pallas_call(
        project_kernel,
        out_shape=[jax.ShapeDtypeStruct((CHUNK, COLS), F32), chunk, chunk, chunk],
        in_specs=[SMEM, VMEM, VMEM, ANY],
        out_specs=[VMEM] * 4,
        compiler_params=PARAMS,
        name="project",
    )(place, mixer_in, w_x, packed)

    def swap(array, d):
        pairs = []
        for i in range(2 * zs):
            y, z = i // zs, i % zs
            pairs.append((i, (y ^ (d >> 1)) * zs + (z ^ (d & 1))))
        return lax.ppermute(array, "mp", pairs)

    groups = [[y * zs + 2 * k + b for k in range(zs // 2)] for y in range(2) for b in range(2)]
    received = [swap(sent[d - 1], d) for d in (1, 2, 3)]
    split = jax.ShapeDtypeStruct((CHUNK // SUB, SUB, COLS), BF)
    added = pl.pallas_call(
        add_four_kernel,
        out_shape=split,
        in_specs=[HBM] * 4 + [ANY],
        out_specs=VMEM,
        scratch_shapes=[pltpu.VMEM((CHUNK, COLS), F32)]
        + [pltpu.VMEM((CHUNK, COLS), BF)] * 3
        + [pltpu.SemaphoreType.DMA((4,))],
        compiler_params=PARAMS,
        name="add_four",
    )(own, *received, got)
    token = jax.ShapeDtypeStruct((8, HD), F32)
    partial = pl.pallas_call(
        cached_kernel,
        out_shape=jax.ShapeDtypeStruct((REQ, RET, channels), BF),
        in_specs=[SMEM, SMEM, SMEM, SMEM, VMEM, VMEM],
        out_specs=VMEM,
        compiler_params=PARAMS,
        name="cached",
    )(tab, place, page_table.T.reshape(-1), kept_len, got, kv_pool.reshape(-1, PAGE, channels))
    block = jax.ShapeDtypeStruct((REQ, 2 * NEW, HD), F32)
    fresh = pl.pallas_call(
        fresh_kernel,
        out_shape=[block, jax.ShapeDtypeStruct((REQ, 8, HD), F32)],
        in_specs=[VMEM] * 2,
        out_specs=[VMEM] * 2,
        compiler_params=PARAMS,
        name="fresh",
    )(queries, kv_new.reshape(rows, channels))
    parts = lax.all_to_all(added, "mp", 0, 0, tiled=True, axis_index_groups=groups)
    summed = pl.pallas_call(
        add_eight_kernel,
        out_shape=split,
        in_specs=[VMEM, ANY],
        out_specs=VMEM,
        compiler_params=PARAMS,
        name="add_eight",
    )(parts, fresh[1])
    whole = lax.all_to_all(summed, "mp", 0, 0, tiled=True, axis_index_groups=groups)
    whole = whole.reshape(CHUNK, COLS)
    others = [swap(whole, d) for d in (1, 2, 3)]

    partial = pl.pallas_call(
        gate_kernel,
        out_shape=jax.ShapeDtypeStruct(partial.shape, BF),
        in_specs=[ANY] * 4,
        out_specs=ANY,
        input_output_aliases={0: 0},
        compiler_params=PARAMS,
        name="gate",
    )(partial, *others)
    back = lax.all_to_all(partial, "req", 0, 0, tiled=True)

    mixer_out, state_out, done = pl.pallas_call(
        scan_kernel,
        out_shape=[
            jax.ShapeDtypeStruct((rows, channels), BF),
            jax.ShapeDtypeStruct((REQ * NS, channels), F32),
            token,
        ],
        in_specs=[SMEM] * 4 + [VMEM] * 4 + [HBM] + [VMEM] * 3 + [HBM] * 3,
        out_specs=[VMEM] * 3,
        scratch_shapes=[
            pltpu.VMEM((channels // HD, rows, HD), F32),
            pltpu.VMEM((channels // HD, rows, HD), F32),
            pltpu.VMEM((rows, COLS - RANK), F32),
            pltpu.VMEM((channels // HD, rows, HD), F32),
            pltpu.VMEM((NS * 8, channels), F32),
            pltpu.VMEM((channels // HD, REQ * NS, HD), F32),
            pltpu.VMEM(w_dt.shape, BF),
            pltpu.VMEM((rows, channels), BF),
            pltpu.VMEM((rows, channels), BF),
            pltpu.VMEM(got.shape, BF),
            pltpu.SemaphoreType.DMA((4,)),
        ],
        compiler_params=PARAMS,
        name="scan",
    )(
        place, tab, cache_index, new_len, whole, *others, w_dt, b_dt.reshape(1, -1), a_rate,
        d_skip.reshape(1, -1), mixer_in, gate_in, got,
    )
    attn_out = pl.pallas_call(
        combine_kernel,
        out_shape=jax.ShapeDtypeStruct((rows, channels), BF),
        in_specs=[SMEM] * 4 + [VMEM] * 3 + [ANY],
        out_specs=VMEM,
        compiler_params=PARAMS,
        name="combine",
    )(place, tab, cache_index, new_len, *fresh, back, done)
    return attn_out, mixer_out, state_out.reshape(REQ, NS, channels)


def solution(mesh):
    placed = (
        P("req", "mp"),
        P("req", "mp", None),
        P("req", None, "mp", None),
        P("req", None, "mp"),
        P("req", "mp"),
        P("req", "mp"),
        P("mp", None),
        P(None, "mp"),
        P("mp"),
        P(None, "mp"),
        P("mp"),
        P(),
        P(),
        P(),
        P(),
    )
    return jax.shard_map(
        on_device,
        mesh=mesh,
        in_specs=placed,
        out_specs=(P("req", "mp"), P("req", "mp"), P("req", None, "mp")),
        check_vma=False,
    )
```

```python
import functools

import jax
import jax.numpy as jnp
from jax import lax
from jax.experimental import pallas as pl
from jax.experimental.pallas import tpu as pltpu
from jax.sharding import PartitionSpec as P

BF = jnp.bfloat16
F32 = jnp.float32
LOG2E = 1.4426950408889634

REQ = 16
NEW = 32
HD = 128
PAGES = 16
PAGE = 16
KEEP = PAGES * PAGE
NS = 16
RANK = 512
COLS = 640
CHUNK = 128
BC = 2 * NS
SUB = 16
STAT = 64
RET = 72
SEND = 96

VMEM = pl.BlockSpec(memory_space=pltpu.VMEM)
ANY = pl.BlockSpec(memory_space=pl.ANY)
HBM = pl.BlockSpec(memory_space=pltpu.HBM)
SMEM = pl.BlockSpec(memory_space=pltpu.SMEM)
SMALL = pltpu.CompilerParams(vmem_limit_bytes=12 * 1024 * 1024)
PARAMS = pltpu.CompilerParams(vmem_limit_bytes=60 * 1024 * 1024)


def tail_of(rest):
    lane = lax.broadcasted_iota(jnp.int32, rest.shape, 1)
    high = rest.astype(BF).astype(F32)
    low = pltpu.roll(rest - high, BC, 1)
    return jnp.where(lane < BC, high, jnp.where(lane < 2 * BC, low, 0.0))


def whole_tail(tail):
    return tail + pltpu.roll(tail, tail.shape[1] - BC, 1)


def fetch(pairs, sems):
    copies = [pltpu.make_async_copy(a, b, sems.at[i]) for i, (a, b) in enumerate(pairs)]
    for copy in copies:
        copy.start()
    return copies


def pack_kernel(tab, entries_hbm, q_hbm, cache_hbm, out_ref, entries, q_ref, cache_ref, sems):
    copies = fetch([(entries_hbm, entries), (q_hbm, q_ref), (cache_hbm, cache_ref)], sems)
    for copy in copies:
        copy.wait()
    for p in range(REQ):
        for k in range(2):
            slot = tab[k * REQ + p]
            out_ref[p, k * NEW : (k + 1) * NEW, :] = q_ref[
                pl.ds(pl.multiple_of(slot * NEW, NEW), NEW), :
            ]
            entry = entries[p * REQ + tab[(2 + k) * REQ + p]] & (REQ - 1)
            out_ref[p, 2 * NEW + k * NS : 2 * NEW + (k + 1) * NS, :] = cache_ref[entry].astype(BF)


def project_kernel(place, x_ref, w_ref, after, own_ref, *sent):
    for d in range(4):
        first = pl.multiple_of((place[0] ^ d) * CHUNK, CHUNK)
        rows = x_ref[pl.ds(first, CHUNK), :]
        low = jnp.dot(rows, w_ref[:, :RANK], preferred_element_type=F32)
        rest = jnp.dot(rows, w_ref[:, RANK:], preferred_element_type=F32)
        rest = jnp.concatenate([rest, jnp.zeros((CHUNK, COLS - RANK - BC), F32)], axis=1)
        if d == 0:
            own_ref[:, :RANK] = low
            own_ref[:, RANK:] = rest
        else:
            sent[d - 1][:, :RANK] = low.astype(BF)
            sent[d - 1][:, RANK:] = tail_of(rest).astype(BF)


def add_four_kernel(own_hbm, h1, h2, h3, after, also, out_ref, own_ref, r1, r2, r3, sems):
    for copy in fetch([(own_hbm, own_ref), (h1, r1), (h2, r2), (h3, r3)], sems):
        copy.wait()
    low = own_ref[:, :RANK]
    tail = jnp.zeros((CHUNK, COLS - RANK), F32)
    for r in (r1, r2, r3):
        low = low + r[:, :RANK].astype(F32)
        tail = tail + r[:, RANK:].astype(F32)
    rest = own_ref[:, RANK:] + whole_tail(tail)
    low = low.astype(BF)
    tail = tail_of(rest).astype(BF)
    for k in range(CHUNK // SUB):
        out_ref[k, :, :RANK] = low[k * SUB : (k + 1) * SUB]
        out_ref[k, :, RANK:] = tail[k * SUB : (k + 1) * SUB]


def add_eight_kernel(parts, after, out_ref):
    total = parts[0].astype(F32)
    for k in range(1, CHUNK // SUB):
        total = total + parts[k].astype(F32)
    low = total[:, :RANK].astype(BF)
    tail = tail_of(whole_tail(total[:, RANK:])).astype(BF)
    for k in range(CHUNK // SUB):
        out_ref[k, :, :RANK] = low
        out_ref[k, :, RANK:] = tail


def gate_kernel(partial, after, out):
    pass


def heads_down(block):
    return jnp.concatenate([block[:, :HD], block[:, HD:]], axis=0)


def cached_kernel(tab, place, table, kept, got_ref, pool_ref, out_ref, done_ref):
    done_ref[...] = jnp.zeros(done_ref.shape, F32)
    row = lax.broadcasted_iota(jnp.int32, (2 * NEW, HD), 0)
    lane = lax.broadcasted_iota(jnp.int32, (2 * NEW, HD), 1)
    key = lax.broadcasted_iota(jnp.int32, (2 * NEW, KEEP), 1)
    base = place[1] * (REQ * PAGES)

    def one_peer(p, carry):
        @pl.when(tab[4 * REQ + p] > 0)
        def _():
            stats = []
            for k in range(2):
                slot = p * REQ + tab[(2 + k) * REQ + p]
                pages = [pool_ref[table[t * REQ * REQ + slot] - base] for t in range(PAGES)]
                rows = jnp.concatenate(pages, axis=0)
                q = heads_down(got_ref[p, k * NEW : (k + 1) * NEW, :])
                s = lax.dot_general(
                    q, rows[:, :HD], (((1,), (1,)), ((), ())), preferred_element_type=F32
                ) * (HD**-0.5)
                s = jnp.where(key < kept[slot], s, -1e30)
                top = jnp.max(s, axis=1, keepdims=True)
                w = jnp.exp(s - top)
                total = jnp.sum(w, axis=1, keepdims=True)
                o = jnp.dot(w.astype(BF), rows[:, HD:], preferred_element_type=F32) / total
                out_ref[p, k * NEW : (k + 1) * NEW, :] = jnp.concatenate(
                    [o[:NEW], o[NEW:]], axis=1
                ).astype(BF)
                lse = top + jnp.log(total)
                stats.append(jnp.sum(jnp.where(row == lane, lse, 0.0), axis=0, keepdims=True))
            flat = jnp.concatenate(stats, axis=0)
            hi = flat.astype(BF).astype(F32)
            mid = (flat - hi).astype(BF).astype(F32)
            low = flat - hi - mid
            none = jnp.zeros((6, HD), F32)
            left = jnp.concatenate([hi, low, none[:4]], axis=0)
            right = jnp.concatenate([mid, none], axis=0)
            out_ref[p, STAT:RET, :] = jnp.concatenate([left, right], axis=1).astype(BF)

        return carry

    lax.fori_loop(0, REQ, one_peer, 0)


def fresh_kernel(q_ref, kv_ref, out_ref, stat_ref):
    row = lax.broadcasted_iota(jnp.int32, (2 * NEW, HD), 0)
    lane = lax.broadcasted_iota(jnp.int32, (2 * NEW, HD), 1)
    query = lax.broadcasted_iota(jnp.int32, (2 * NEW, NEW), 0) & (NEW - 1)
    key = lax.broadcasted_iota(jnp.int32, (2 * NEW, NEW), 1)

    def one_slot(i, carry):
        first = pl.multiple_of(i * NEW, NEW)
        q = heads_down(q_ref[pl.ds(first, NEW), :])
        rows = kv_ref[pl.ds(first, NEW), :]
        s = lax.dot_general(
            q, rows[:, :HD], (((1,), (1,)), ((), ())), preferred_element_type=F32
        ) * (HD**-0.5)
        s = jnp.where(key <= query, s, -1e30)
        top = jnp.max(s, axis=1, keepdims=True)
        w = jnp.exp(s - top)
        total = jnp.sum(w, axis=1, keepdims=True)
        out_ref[i] = jnp.dot(w.astype(BF), rows[:, HD:], preferred_element_type=F32) / total
        lse = top + jnp.log(total)
        flat = jnp.sum(jnp.where(row == lane, lse, 0.0), axis=0, keepdims=True)
        stat_ref[i] = jnp.broadcast_to(flat, (8, HD))
        return carry

    lax.fori_loop(0, REQ, one_slot, 0, unroll=4)


def combine_kernel(place, tab, entries, fresh_len, part_ref, stat_ref, got_ref, after, out_ref):
    row = lax.broadcasted_iota(jnp.int32, (2 * NEW, HD), 0)
    lane = lax.broadcasted_iota(jnp.int32, (2 * NEW, HD), 1)
    spot = lax.broadcasted_iota(jnp.int32, (NEW, 2 * HD), 0)

    def one_slot(i, carry):
        first = pl.multiple_of(i * NEW, NEW)
        owner = entries[place[1] * REQ + i] // REQ
        second = (tab[REQ + owner] == i).astype(jnp.int32)
        old = heads_down(
            got_ref[owner, pl.ds(pl.multiple_of(second * NEW, NEW), NEW), :]
        ).astype(F32)
        stats = got_ref[owner, STAT:RET, :].astype(F32)
        exact = stats[0:2, :HD] + stats[0:2, HD:] + stats[2:4, :HD]
        lse_old = jnp.where(second > 0, exact[1:2], exact[0:1])
        lse = stat_ref[i, 0:1, :]
        most = jnp.maximum(lse_old, lse)
        weight_old = jnp.exp(lse_old - most)
        weight = jnp.exp(lse - most)
        share_old = weight_old / (weight_old + weight)
        share_old = jnp.sum(jnp.where(row == lane, share_old, 0.0), axis=1, keepdims=True)
        share = weight / (weight_old + weight)
        share = jnp.sum(jnp.where(row == lane, share, 0.0), axis=1, keepdims=True)
        o = old * share_old + part_ref[i] * share
        o = jnp.concatenate([o[:NEW], o[NEW:]], axis=1)
        live = spot < fresh_len[place[1] * REQ + i]
        out_ref[pl.ds(first, NEW), :] = jnp.where(live, o, 0.0).astype(BF)
        return carry

    lax.fori_loop(0, REQ, one_slot, 0, unroll=4)


def scan_kernel(
    place, tab, entries, fresh_len, low_ref, wdt_hbm, b_ref, a_ref, d_ref, x_hbm, g_hbm, got_hbm,
    out_ref, state_ref, done_ref, dt_s, u_s, bc_s, y_s, a_s, h_s, wdt_ref, x_ref, g_ref, got_ref, sems,
):
    copies = fetch(
        [(wdt_hbm, wdt_ref), (x_hbm, x_ref), (got_hbm, got_ref), (g_hbm, g_ref)], sems
    )
    done_ref[...] = jnp.zeros(done_ref.shape, F32)
    channels = x_ref.shape[1]
    halves = [slice(c * HD, (c + 1) * HD) for c in range(channels // HD)]
    step = lax.broadcasted_iota(jnp.int32, (NEW, channels), 0)
    for n in range(NS):
        a_s[n * 8 : (n + 1) * 8, :] = jnp.broadcast_to(a_ref[n : n + 1, :] * (-LOG2E), (8, channels))
    copies[0].wait()
    copies[1].wait()
    for member in range(4):
        part = low_ref[member]
        first = member * CHUNK
        pre = jnp.dot(part[:, :RANK], wdt_ref[...], preferred_element_type=F32) + b_ref[...]
        dt = jnp.maximum(pre, 0.0) + jnp.log1p(jnp.exp(-jnp.abs(pre)))
        bc_s[pl.ds(first, CHUNK), :] = whole_tail(part[:, RANK:].astype(F32))
        for j in range(CHUNK // NEW):
            here = first + j * NEW
            live = step < fresh_len[place[1] * REQ + member * (CHUNK // NEW) + j]
            masked = jnp.where(live, dt[j * NEW : (j + 1) * NEW], 0.0)
            drive = masked * x_ref[pl.ds(here, NEW), :].astype(F32)
            for c, half in enumerate(halves):
                dt_s[c, pl.ds(here, NEW), :] = masked[:, half]
                u_s[c, pl.ds(here, NEW), :] = drive[:, half]
    copies[2].wait()
    for i in range(REQ):
        owner = entries[place[1] * REQ + i] // REQ
        second = (tab[REQ + owner] == i).astype(jnp.int32)
        start = pl.multiple_of(2 * NEW + second * NS, NS)
        state = got_ref[owner, pl.ds(start, NS), :].astype(F32)
        for c, half in enumerate(halves):
            h_s[c, i * NS : (i + 1) * NS, :] = state[:, half]
    for g in range(2):
        begin = g * 8 * NS
        h0 = tuple(
            tuple(h_s[c, pl.ds(begin + n, 8, stride=NS), :] for c in range(len(halves)))
            for n in range(NS)
        )

        def one_step(i, hs):
            rows = pl.ds(g * 8 * NEW + i, 8, stride=NEW)
            dt = [dt_s[c, rows, :] for c in range(len(halves))]
            u = [u_s[c, rows, :] for c in range(len(halves))]
            bc = bc_s[rows, :]
            y = [0.0] * len(halves)
            new = []
            for n in range(NS):
                b_in = jnp.broadcast_to(bc[:, n : n + 1], (8, HD))
                c_out = jnp.broadcast_to(bc[:, NS + n : NS + n + 1], (8, HD))
                pair = []
                for c, half in enumerate(halves):
                    decay = jnp.exp2(dt[c] * a_s[n * 8 : (n + 1) * 8, half])
                    h = decay * hs[n][c] + u[c] * b_in
                    y[c] = y[c] + h * c_out
                    pair.append(h)
                new.append(tuple(pair))
            for c in range(len(halves)):
                y_s[c, rows, :] = y[c]
            return tuple(new)

        hs = lax.fori_loop(0, NEW, one_step, h0, unroll=8)
        for n in range(NS):
            for c in range(len(halves)):
                h_s[c, pl.ds(begin + n, 8, stride=NS), :] = hs[n][c]
    for c, half in enumerate(halves):
        state_ref[:, half] = h_s[c]
    copies[3].wait()
    for i in range(REQ):
        rows = slice(i * NEW, (i + 1) * NEW)
        for c, half in enumerate(halves):
            gate = g_ref[rows, half].astype(F32)
            y = y_s[c, rows, :] + d_ref[:, half] * x_ref[rows, half].astype(F32)
            y = y * (gate * jax.nn.sigmoid(gate))
            out_ref[rows, half] = jnp.where(step[:, half] < fresh_len[place[1] * REQ + i], y, 0.0).astype(BF)


def on_device(
    queries, kv_new, kv_pool, ssm_cache, mixer_in, gate_in, w_x, w_dt, b_dt, a_rate, d_skip,
    kept_len, new_len, cache_index, page_table,
):
    rows, channels = mixer_in.shape
    me = lax.axis_index("req")
    at = lax.axis_index("mp")
    zs = lax.axis_size("mp") // 2
    member = (at // zs) * 2 + (at & 1)
    place = jnp.stack([member, me]).astype(jnp.int32)

    slots = jnp.arange(REQ * REQ, dtype=jnp.int32)[None, :]
    peers = jnp.arange(REQ, dtype=jnp.int32)[:, None]
    owners = (cache_index // REQ)[None, :]

    def ends(match):
        first = jnp.min(jnp.where(match, slots & (REQ - 1), REQ - 1), axis=1)
        last = jnp.max(jnp.where(match, slots & (REQ - 1), -1), axis=1)
        return first, jnp.maximum(last, 0), (last >= 0).astype(jnp.int32)

    q_first, q_last, _ = ends((owners == peers) & (slots // REQ == me))
    s_first, s_last, active = ends((owners == me) & (slots // REQ == peers))
    tab = jnp.concatenate([q_first, q_last, s_first, s_last, active])

    packed = pl.pallas_call(
        pack_kernel,
        out_shape=jax.ShapeDtypeStruct((REQ, SEND, channels), BF),
        in_specs=[SMEM, HBM, HBM, HBM],
        out_specs=VMEM,
        scratch_shapes=[
            pltpu.SMEM(cache_index.shape, jnp.int32),
            pltpu.VMEM(queries.shape, BF),
            pltpu.VMEM(ssm_cache.shape, F32),
            pltpu.SemaphoreType.DMA((3,)),
        ],
        compiler_params=PARAMS,
        name="pack",
    )(tab, cache_index, queries, ssm_cache)
    got = lax.all_to_all(packed, "req", 0, 0, tiled=True)

    chunk = jax.ShapeDtypeStruct((CHUNK, COLS), BF)
    own, *sent = pl.pallas_call(
        project_kernel,
        out_shape=[jax.ShapeDtypeStruct((CHUNK, COLS), F32), chunk, chunk, chunk],
        in_specs=[SMEM, VMEM, VMEM, ANY],
        out_specs=[VMEM] * 4,
        compiler_params=PARAMS,
        name="project",
    )(place, mixer_in, w_x, packed)

    def swap(array, d):
        pairs = []
        for i in range(2 * zs):
            y, z = i // zs, i % zs
            pairs.append((i, (y ^ (d >> 1)) * zs + (z ^ (d & 1))))
        return lax.ppermute(array, "mp", pairs)

    quads = [[y * zs + 2 * k + b for y in range(2) for b in range(2)] for k in range(zs // 2)]
    groups = [[y * zs + 2 * k + b for k in range(zs // 2)] for y in range(2) for b in range(2)]
    received = [swap(sent[d - 1], d) for d in (1, 2, 3)]
    split = jax.ShapeDtypeStruct((CHUNK // SUB, SUB, COLS), BF)
    block = jax.ShapeDtypeStruct((REQ, 2 * NEW, HD), F32)
    fresh = pl.pallas_call(
        fresh_kernel,
        out_shape=[block, jax.ShapeDtypeStruct((REQ, 8, HD), F32)],
        in_specs=[VMEM] * 2,
        out_specs=[VMEM] * 2,
        compiler_params=PARAMS,
        name="fresh",
    )(queries, kv_new.reshape(rows, channels))
    added = pl.pallas_call(
        add_four_kernel,
        out_shape=split,
        in_specs=[HBM] * 4 + [ANY] * 2,
        out_specs=VMEM,
        scratch_shapes=[pltpu.VMEM((CHUNK, COLS), F32)]
        + [pltpu.VMEM((CHUNK, COLS), BF)] * 3
        + [pltpu.SemaphoreType.DMA((4,))],
        compiler_params=PARAMS,
        name="add_four",
    )(own, *received, got, fresh[1])
    token = jax.ShapeDtypeStruct((8, HD), F32)
    partial, cached = pl.pallas_call(
        cached_kernel,
        out_shape=[jax.ShapeDtypeStruct((REQ, RET, channels), BF), token],
        in_specs=[SMEM, SMEM, SMEM, SMEM, VMEM, VMEM],
        out_specs=[VMEM] * 2,
        compiler_params=SMALL,
        name="cached",
    )(tab, place, page_table.T.reshape(-1), kept_len, got, kv_pool.reshape(-1, PAGE, channels))
    parts = lax.all_to_all(added, "mp", 0, 0, tiled=True, axis_index_groups=groups)
    summed = pl.pallas_call(
        add_eight_kernel,
        out_shape=split,
        in_specs=[VMEM, ANY],
        out_specs=VMEM,
        compiler_params=SMALL,
        name="add_eight",
    )(parts, cached)
    whole = lax.all_to_all(summed, "mp", 0, 0, tiled=True, axis_index_groups=groups)
    whole = jnp.broadcast_to(whole.reshape(1, CHUNK, COLS), (4, CHUNK, COLS))
    whole = lax.all_to_all(whole, "mp", 0, 0, tiled=True, axis_index_groups=quads)

    partial = pl.pallas_call(
        gate_kernel,
        out_shape=jax.ShapeDtypeStruct(partial.shape, BF),
        in_specs=[ANY] * 2,
        out_specs=ANY,
        input_output_aliases={0: 0},
        compiler_params=PARAMS,
        name="gate",
    )(partial, whole)
    back = lax.all_to_all(partial, "req", 0, 0, tiled=True)

    mixer_out, state_out, done = pl.pallas_call(
        scan_kernel,
        out_shape=[
            jax.ShapeDtypeStruct((rows, channels), BF),
            jax.ShapeDtypeStruct((REQ * NS, channels), F32),
            token,
        ],
        in_specs=[SMEM] * 4 + [VMEM, HBM] + [VMEM] * 3 + [HBM] * 3,
        out_specs=[VMEM] * 3,
        scratch_shapes=[
            pltpu.VMEM((channels // HD, rows, HD), F32),
            pltpu.VMEM((channels // HD, rows, HD), F32),
            pltpu.VMEM((rows, COLS - RANK), F32),
            pltpu.VMEM((channels // HD, rows, HD), F32),
            pltpu.VMEM((NS * 8, channels), F32),
            pltpu.VMEM((channels // HD, REQ * NS, HD), F32),
            pltpu.VMEM(w_dt.shape, BF),
            pltpu.VMEM((rows, channels), BF),
            pltpu.VMEM((rows, channels), BF),
            pltpu.VMEM(got.shape, BF),
            pltpu.SemaphoreType.DMA((4,)),
        ],
        compiler_params=PARAMS,
        name="scan",
    )(
        place, tab, cache_index, new_len, whole, w_dt, b_dt.reshape(1, -1), a_rate,
        d_skip.reshape(1, -1), mixer_in, gate_in, got,
    )
    attn_out = pl.pallas_call(
        combine_kernel,
        out_shape=jax.ShapeDtypeStruct((rows, channels), BF),
        in_specs=[SMEM] * 4 + [VMEM] * 3 + [ANY],
        out_specs=VMEM,
        compiler_params=PARAMS,
        name="combine",
    )(place, tab, cache_index, new_len, *fresh, back, done)
    return attn_out, mixer_out, state_out.reshape(REQ, NS, channels)


def solution(mesh):
    placed = (
        P("req", "mp"),
        P("req", "mp", None),
        P("req", None, "mp", None),
        P("req", None, "mp"),
        P("req", "mp"),
        P("req", "mp"),
        P("mp", None),
        P(None, "mp"),
        P("mp"),
        P(None, "mp"),
        P("mp"),
        P(),
        P(),
        P(),
        P(),
    )
    return jax.shard_map(
        on_device,
        mesh=mesh,
        in_specs=placed,
        out_specs=(P("req", "mp"), P("req", "mp"), P("req", None, "mp")),
        check_vma=False,
    )
```

```python
import functools

import jax
import jax.numpy as jnp
from jax import lax
from jax.experimental import pallas as pl
from jax.experimental.pallas import tpu as pltpu
from jax.sharding import PartitionSpec as P

BF = jnp.bfloat16
F32 = jnp.float32
LOG2E = 1.4426950408889634

REQ = 16
NEW = 32
HD = 128
PAGES = 16
PAGE = 16
KEEP = PAGES * PAGE
NS = 16
RANK = 512
COLS = 640
CHUNK = 128
BC = 2 * NS
SUB = 16
STAT = 64
RET = 72
SEND = 96
TABLE = 6 * REQ

VMEM = pl.BlockSpec(memory_space=pltpu.VMEM)
ANY = pl.BlockSpec(memory_space=pl.ANY)
HBM = pl.BlockSpec(memory_space=pltpu.HBM)
SMEM = pl.BlockSpec(memory_space=pltpu.SMEM)
SMALL = pltpu.CompilerParams(vmem_limit_bytes=12 * 1024 * 1024)
PARAMS = pltpu.CompilerParams(vmem_limit_bytes=60 * 1024 * 1024)


def tail_of(rest):
    lane = lax.broadcasted_iota(jnp.int32, rest.shape, 1)
    high = rest.astype(BF).astype(F32)
    low = pltpu.roll(rest - high, BC, 1)
    return jnp.where(lane < BC, high, jnp.where(lane < 2 * BC, low, 0.0))


def whole_tail(tail):
    return tail + pltpu.roll(tail, tail.shape[1] - BC, 1)


def fetch(pairs, sems):
    copies = [pltpu.make_async_copy(a, b, sems.at[i]) for i, (a, b) in enumerate(pairs)]
    for copy in copies:
        copy.start()
    return copies


def pack_kernel(entries_hbm, q_hbm, cache_hbm, out_ref, tab, entries, q_ref, cache_ref, sems):
    copies = fetch([(entries_hbm, entries), (q_hbm, q_ref), (cache_hbm, cache_ref)], sems)
    me = lax.axis_index("req")
    for i in range(TABLE):
        tab[i] = 0
    copies[0].wait()
    for i in range(REQ):
        owner = entries[me * REQ + i] // REQ
        count = tab[5 * REQ + owner]
        tab[jnp.minimum(count, 1) * REQ + owner] = i
        tab[5 * REQ + owner] = count + 1

    def one_peer(p, carry):
        count = jnp.int32(0)
        for i in range(REQ):
            match = entries[p * REQ + i] // REQ == me
            tab[jnp.where(match, (2 + jnp.minimum(count, 1)) * REQ, 5 * REQ) + p] = i
            count = count + match.astype(jnp.int32)
        tab[4 * REQ + p] = count
        return carry

    lax.fori_loop(0, REQ, one_peer, 0)
    copies[1].wait()
    copies[2].wait()
    for p in range(REQ):
        for k in range(2):
            slot = tab[k * REQ + p]
            out_ref[p, k * NEW : (k + 1) * NEW, :] = q_ref[
                pl.ds(pl.multiple_of(slot * NEW, NEW), NEW), :
            ]
            entry = entries[p * REQ + tab[(2 + k) * REQ + p]] & (REQ - 1)
            out_ref[p, 2 * NEW + k * NS : 2 * NEW + (k + 1) * NS, :] = cache_ref[entry].astype(BF)


def project_kernel(x_ref, w_ref, after, own_ref, *sent):
    at = lax.axis_index("mp")
    member = (at // (lax.axis_size("mp") // 2)) * 2 + (at & 1)
    for d in range(4):
        first = pl.multiple_of((member ^ d) * CHUNK, CHUNK)
        rows = x_ref[pl.ds(first, CHUNK), :]
        low = jnp.dot(rows, w_ref[:, :RANK], preferred_element_type=F32)
        rest = jnp.dot(rows, w_ref[:, RANK:], preferred_element_type=F32)
        rest = jnp.concatenate([rest, jnp.zeros((CHUNK, COLS - RANK - BC), F32)], axis=1)
        if d == 0:
            own_ref[:, :RANK] = low
            own_ref[:, RANK:] = rest
        else:
            sent[d - 1][:, :RANK] = low.astype(BF)
            sent[d - 1][:, RANK:] = tail_of(rest).astype(BF)


def add_four_kernel(own_ref, r1, r2, r3, after, out_ref):
    low = own_ref[:, :RANK]
    tail = jnp.zeros((CHUNK, COLS - RANK), F32)
    for r in (r1, r2, r3):
        low = low + r[:, :RANK].astype(F32)
        tail = tail + r[:, RANK:].astype(F32)
    rest = own_ref[:, RANK:] + whole_tail(tail)
    low = low.astype(BF)
    tail = tail_of(rest).astype(BF)
    for k in range(CHUNK // SUB):
        out_ref[k, :, :RANK] = low[k * SUB : (k + 1) * SUB]
        out_ref[k, :, RANK:] = tail[k * SUB : (k + 1) * SUB]


def add_eight_kernel(parts, after, out_ref):
    total = parts[0].astype(F32)
    for k in range(1, CHUNK // SUB):
        total = total + parts[k].astype(F32)
    low = total[:, :RANK].astype(BF)
    tail = tail_of(whole_tail(total[:, RANK:])).astype(BF)
    for k in range(CHUNK // SUB):
        out_ref[k, :, :RANK] = low
        out_ref[k, :, RANK:] = tail


def gate_kernel(partial, after, out):
    pass


def heads_down(block):
    return jnp.concatenate([block[:, :HD], block[:, HD:]], axis=0)


def cached_kernel(tab, table, kept, got_ref, pool_ref, out_ref, done_ref):
    done_ref[...] = jnp.zeros(done_ref.shape, F32)
    row = lax.broadcasted_iota(jnp.int32, (2 * NEW, HD), 0)
    lane = lax.broadcasted_iota(jnp.int32, (2 * NEW, HD), 1)
    key = lax.broadcasted_iota(jnp.int32, (2 * NEW, KEEP), 1)
    base = lax.axis_index("req") * (REQ * PAGES)

    def one_peer(p, carry):
        @pl.when(tab[4 * REQ + p] > 0)
        def _():
            stats = []
            for k in range(2):
                slot = p * REQ + tab[(2 + k) * REQ + p]
                pages = [pool_ref[table[t * REQ * REQ + slot] - base] for t in range(PAGES)]
                rows = jnp.concatenate(pages, axis=0)
                q = heads_down(got_ref[p, k * NEW : (k + 1) * NEW, :])
                s = lax.dot_general(
                    q, rows[:, :HD], (((1,), (1,)), ((), ())), preferred_element_type=F32
                ) * (HD**-0.5)
                s = jnp.where(key < kept[slot], s, -1e30)
                top = jnp.max(s, axis=1, keepdims=True)
                w = jnp.exp(s - top)
                total = jnp.sum(w, axis=1, keepdims=True)
                o = jnp.dot(w.astype(BF), rows[:, HD:], preferred_element_type=F32) / total
                out_ref[p, k * NEW : (k + 1) * NEW, :] = jnp.concatenate(
                    [o[:NEW], o[NEW:]], axis=1
                ).astype(BF)
                lse = top + jnp.log(total)
                stats.append(jnp.sum(jnp.where(row == lane, lse, 0.0), axis=0, keepdims=True))
            flat = jnp.concatenate(stats, axis=0)
            hi = flat.astype(BF).astype(F32)
            mid = (flat - hi).astype(BF).astype(F32)
            low = flat - hi - mid
            none = jnp.zeros((6, HD), F32)
            left = jnp.concatenate([hi, low, none[:4]], axis=0)
            right = jnp.concatenate([mid, none], axis=0)
            out_ref[p, STAT:RET, :] = jnp.concatenate([left, right], axis=1).astype(BF)

        return carry

    lax.fori_loop(0, REQ, one_peer, 0)


def fresh_kernel(q_ref, kv_ref, out_ref, stat_ref):
    row = lax.broadcasted_iota(jnp.int32, (2 * NEW, HD), 0)
    lane = lax.broadcasted_iota(jnp.int32, (2 * NEW, HD), 1)
    query = lax.broadcasted_iota(jnp.int32, (2 * NEW, NEW), 0) & (NEW - 1)
    key = lax.broadcasted_iota(jnp.int32, (2 * NEW, NEW), 1)

    def one_slot(i, carry):
        first = pl.multiple_of(i * NEW, NEW)
        q = heads_down(q_ref[pl.ds(first, NEW), :])
        rows = kv_ref[pl.ds(first, NEW), :]
        s = lax.dot_general(
            q, rows[:, :HD], (((1,), (1,)), ((), ())), preferred_element_type=F32
        ) * (HD**-0.5)
        s = jnp.where(key <= query, s, -1e30)
        top = jnp.max(s, axis=1, keepdims=True)
        w = jnp.exp(s - top)
        total = jnp.sum(w, axis=1, keepdims=True)
        out_ref[i] = jnp.dot(w.astype(BF), rows[:, HD:], preferred_element_type=F32) / total
        lse = top + jnp.log(total)
        flat = jnp.sum(jnp.where(row == lane, lse, 0.0), axis=0, keepdims=True)
        stat_ref[i] = jnp.broadcast_to(flat, (8, HD))
        return carry

    lax.fori_loop(0, REQ, one_slot, 0, unroll=4)


def combine_kernel(tab, entries, fresh_len, part_ref, stat_ref, got_ref, after, out_ref):
    base = lax.axis_index("req") * REQ
    row = lax.broadcasted_iota(jnp.int32, (2 * NEW, HD), 0)
    lane = lax.broadcasted_iota(jnp.int32, (2 * NEW, HD), 1)
    spot = lax.broadcasted_iota(jnp.int32, (NEW, 2 * HD), 0)

    def one_slot(i, carry):
        first = pl.multiple_of(i * NEW, NEW)
        owner = entries[base + i] // REQ
        second = (tab[REQ + owner] == i).astype(jnp.int32)
        old = heads_down(
            got_ref[owner, pl.ds(pl.multiple_of(second * NEW, NEW), NEW), :]
        ).astype(F32)
        stats = got_ref[owner, STAT:RET, :].astype(F32)
        exact = stats[0:2, :HD] + stats[0:2, HD:] + stats[2:4, :HD]
        lse_old = jnp.where(second > 0, exact[1:2], exact[0:1])
        lse = stat_ref[i, 0:1, :]
        most = jnp.maximum(lse_old, lse)
        weight_old = jnp.exp(lse_old - most)
        weight = jnp.exp(lse - most)
        share_old = weight_old / (weight_old + weight)
        share_old = jnp.sum(jnp.where(row == lane, share_old, 0.0), axis=1, keepdims=True)
        share = weight / (weight_old + weight)
        share = jnp.sum(jnp.where(row == lane, share, 0.0), axis=1, keepdims=True)
        o = old * share_old + part_ref[i] * share
        o = jnp.concatenate([o[:NEW], o[NEW:]], axis=1)
        live = spot < fresh_len[base + i]
        out_ref[pl.ds(first, NEW), :] = jnp.where(live, o, 0.0).astype(BF)
        return carry

    lax.fori_loop(0, REQ, one_slot, 0, unroll=4)


def scan_kernel(
    tab, entries, fresh_len, low_ref, wdt_hbm, b_ref, a_ref, d_ref, x_hbm, g_hbm, got_hbm,
    out_ref, state_ref, done_ref, dt_s, u_s, bc_s, y_s, a_s, h_s, wdt_ref, x_ref, g_ref, got_ref, sems,
):
    copies = fetch(
        [(wdt_hbm, wdt_ref), (x_hbm, x_ref), (got_hbm, got_ref), (g_hbm, g_ref)], sems
    )
    done_ref[...] = jnp.zeros(done_ref.shape, F32)
    base = lax.axis_index("req") * REQ
    channels = x_ref.shape[1]
    halves = [slice(c * HD, (c + 1) * HD) for c in range(channels // HD)]
    step = lax.broadcasted_iota(jnp.int32, (NEW, channels), 0)
    for n in range(NS):
        a_s[n * 8 : (n + 1) * 8, :] = jnp.broadcast_to(a_ref[n : n + 1, :] * (-LOG2E), (8, channels))
    copies[0].wait()
    copies[1].wait()
    for member in range(4):
        part = low_ref[member]
        first = member * CHUNK
        pre = jnp.dot(part[:, :RANK], wdt_ref[...], preferred_element_type=F32) + b_ref[...]
        dt = jnp.maximum(pre, 0.0) + jnp.log1p(jnp.exp(-jnp.abs(pre)))
        bc_s[pl.ds(first, CHUNK), :] = whole_tail(part[:, RANK:].astype(F32))
        for j in range(CHUNK // NEW):
            here = first + j * NEW
            live = step < fresh_len[base + member * (CHUNK // NEW) + j]
            masked = jnp.where(live, dt[j * NEW : (j + 1) * NEW], 0.0)
            drive = masked * x_ref[pl.ds(here, NEW), :].astype(F32)
            for c, half in enumerate(halves):
                dt_s[c, pl.ds(here, NEW), :] = masked[:, half]
                u_s[c, pl.ds(here, NEW), :] = drive[:, half]
    copies[2].wait()
    for i in range(REQ):
        owner = entries[base + i] // REQ
        second = (tab[REQ + owner] == i).astype(jnp.int32)
        start = pl.multiple_of(2 * NEW + second * NS, NS)
        state = got_ref[owner, pl.ds(start, NS), :].astype(F32)
        for c, half in enumerate(halves):
            h_s[c, i * NS : (i + 1) * NS, :] = state[:, half]
    for g in range(2):
        begin = g * 8 * NS
        h0 = tuple(
            tuple(h_s[c, pl.ds(begin + n, 8, stride=NS), :] for c in range(len(halves)))
            for n in range(NS)
        )

        def one_step(i, hs):
            rows = pl.ds(g * 8 * NEW + i, 8, stride=NEW)
            dt = [dt_s[c, rows, :] for c in range(len(halves))]
            u = [u_s[c, rows, :] for c in range(len(halves))]
            bc = bc_s[rows, :]
            y = [0.0] * len(halves)
            new = []
            for n in range(NS):
                b_in = jnp.broadcast_to(bc[:, n : n + 1], (8, HD))
                c_out = jnp.broadcast_to(bc[:, NS + n : NS + n + 1], (8, HD))
                pair = []
                for c, half in enumerate(halves):
                    decay = jnp.exp2(dt[c] * a_s[n * 8 : (n + 1) * 8, half])
                    h = decay * hs[n][c] + u[c] * b_in
                    y[c] = y[c] + h * c_out
                    pair.append(h)
                new.append(tuple(pair))
            for c in range(len(halves)):
                y_s[c, rows, :] = y[c]
            return tuple(new)

        hs = lax.fori_loop(0, NEW, one_step, h0, unroll=8)
        for n in range(NS):
            for c in range(len(halves)):
                h_s[c, pl.ds(begin + n, 8, stride=NS), :] = hs[n][c]
    for c, half in enumerate(halves):
        state_ref[:, half] = h_s[c]
    copies[3].wait()
    for i in range(REQ):
        rows = slice(i * NEW, (i + 1) * NEW)
        for c, half in enumerate(halves):
            gate = g_ref[rows, half].astype(F32)
            y = y_s[c, rows, :] + d_ref[:, half] * x_ref[rows, half].astype(F32)
            y = y * (gate * jax.nn.sigmoid(gate))
            out_ref[rows, half] = jnp.where(step[:, half] < fresh_len[base + i], y, 0.0).astype(BF)


def on_device(
    queries, kv_new, kv_pool, ssm_cache, mixer_in, gate_in, w_x, w_dt, b_dt, a_rate, d_skip,
    kept_len, new_len, cache_index, page_table,
):
    rows, channels = mixer_in.shape
    zs = lax.axis_size("mp") // 2

    packed, tab = pl.pallas_call(
        pack_kernel,
        out_shape=[
            jax.ShapeDtypeStruct((REQ, SEND, channels), BF),
            jax.ShapeDtypeStruct((TABLE,), jnp.int32),
        ],
        in_specs=[HBM, HBM, HBM],
        out_specs=[VMEM, SMEM],
        scratch_shapes=[
            pltpu.SMEM(cache_index.shape, jnp.int32),
            pltpu.VMEM(queries.shape, BF),
            pltpu.VMEM(ssm_cache.shape, F32),
            pltpu.SemaphoreType.DMA((3,)),
        ],
        compiler_params=PARAMS,
        name="pack",
    )(cache_index, queries, ssm_cache)
    got = lax.all_to_all(packed, "req", 0, 0, tiled=True)

    chunk = jax.ShapeDtypeStruct((CHUNK, COLS), BF)
    own, *sent = pl.pallas_call(
        project_kernel,
        out_shape=[jax.ShapeDtypeStruct((CHUNK, COLS), F32), chunk, chunk, chunk],
        in_specs=[VMEM, VMEM, ANY],
        out_specs=[VMEM] * 4,
        compiler_params=SMALL,
        name="project",
    )(mixer_in, w_x, packed)

    def swap(array, d):
        pairs = []
        for i in range(2 * zs):
            y, z = i // zs, i % zs
            pairs.append((i, (y ^ (d >> 1)) * zs + (z ^ (d & 1))))
        return lax.ppermute(array, "mp", pairs)

    quads = [[y * zs + 2 * k + b for y in range(2) for b in range(2)] for k in range(zs // 2)]
    groups = [[y * zs + 2 * k + b for k in range(zs // 2)] for y in range(2) for b in range(2)]
    received = [swap(sent[d - 1], d) for d in (1, 2, 3)]
    split = jax.ShapeDtypeStruct((CHUNK // SUB, SUB, COLS), BF)
    block = jax.ShapeDtypeStruct((REQ, 2 * NEW, HD), F32)
    fresh = pl.pallas_call(
        fresh_kernel,
        out_shape=[block, jax.ShapeDtypeStruct((REQ, 8, HD), F32)],
        in_specs=[VMEM] * 2,
        out_specs=[VMEM] * 2,
        compiler_params=SMALL,
        name="fresh",
    )(queries, kv_new.reshape(rows, channels))
    added = pl.pallas_call(
        add_four_kernel,
        out_shape=split,
        in_specs=[VMEM] * 4 + [ANY],
        out_specs=VMEM,
        compiler_params=SMALL,
        name="add_four",
    )(own, *received, fresh[1])
    token = jax.ShapeDtypeStruct((8, HD), F32)
    partial, cached = pl.pallas_call(
        cached_kernel,
        out_shape=[jax.ShapeDtypeStruct((REQ, RET, channels), BF), token],
        in_specs=[SMEM, SMEM, SMEM, VMEM, VMEM],
        out_specs=[VMEM] * 2,
        compiler_params=SMALL,
        name="cached",
    )(tab, page_table.T.reshape(-1), kept_len, got, kv_pool.reshape(-1, PAGE, channels))
    parts = lax.all_to_all(added, "mp", 0, 0, tiled=True, axis_index_groups=groups)
    summed = pl.pallas_call(
        add_eight_kernel,
        out_shape=split,
        in_specs=[VMEM, ANY],
        out_specs=VMEM,
        compiler_params=SMALL,
        name="add_eight",
    )(parts, cached)
    whole = lax.all_to_all(summed, "mp", 0, 0, tiled=True, axis_index_groups=groups)
    whole = jnp.broadcast_to(whole.reshape(1, CHUNK, COLS), (4, CHUNK, COLS))
    whole = lax.all_to_all(whole, "mp", 0, 0, tiled=True, axis_index_groups=quads)

    partial = pl.pallas_call(
        gate_kernel,
        out_shape=jax.ShapeDtypeStruct(partial.shape, BF),
        in_specs=[ANY] * 2,
        out_specs=ANY,
        input_output_aliases={0: 0},
        compiler_params=PARAMS,
        name="gate",
    )(partial, whole)
    back = lax.all_to_all(partial, "req", 0, 0, tiled=True)

    mixer_out, state_out, done = pl.pallas_call(
        scan_kernel,
        out_shape=[
            jax.ShapeDtypeStruct((rows, channels), BF),
            jax.ShapeDtypeStruct((REQ * NS, channels), F32),
            token,
        ],
        in_specs=[SMEM] * 3 + [VMEM, HBM] + [VMEM] * 3 + [HBM] * 3,
        out_specs=[VMEM] * 3,
        scratch_shapes=[
            pltpu.VMEM((channels // HD, rows, HD), F32),
            pltpu.VMEM((channels // HD, rows, HD), F32),
            pltpu.VMEM((rows, COLS - RANK), F32),
            pltpu.VMEM((channels // HD, rows, HD), F32),
            pltpu.VMEM((NS * 8, channels), F32),
            pltpu.VMEM((channels // HD, REQ * NS, HD), F32),
            pltpu.VMEM(w_dt.shape, BF),
            pltpu.VMEM((rows, channels), BF),
            pltpu.VMEM((rows, channels), BF),
            pltpu.VMEM(got.shape, BF),
            pltpu.SemaphoreType.DMA((4,)),
        ],
        compiler_params=PARAMS,
        name="scan",
    )(
        tab, cache_index, new_len, whole, w_dt, b_dt.reshape(1, -1), a_rate,
        d_skip.reshape(1, -1), mixer_in, gate_in, got,
    )
    attn_out = pl.pallas_call(
        combine_kernel,
        out_shape=jax.ShapeDtypeStruct((rows, channels), BF),
        in_specs=[SMEM] * 3 + [VMEM] * 3 + [ANY],
        out_specs=VMEM,
        compiler_params=SMALL,
        name="combine",
    )(tab, cache_index, new_len, *fresh, back, done)
    return attn_out, mixer_out, state_out.reshape(REQ, NS, channels)


def solution(mesh):
    placed = (
        P("req", "mp"),
        P("req", "mp", None),
        P("req", None, "mp", None),
        P("req", None, "mp"),
        P("req", "mp"),
        P("req", "mp"),
        P("mp", None),
        P(None, "mp"),
        P("mp"),
        P(None, "mp"),
        P("mp"),
        P(),
        P(),
        P(),
        P(),
    )
    return jax.shard_map(
        on_device,
        mesh=mesh,
        in_specs=placed,
        out_specs=(P("req", "mp"), P("req", "mp"), P("req", None, "mp")),
        check_vma=False,
    )
```

```python
import functools

import jax
import jax.numpy as jnp
from jax import lax
from jax.experimental import pallas as pl
from jax.experimental.pallas import tpu as pltpu
from jax.sharding import PartitionSpec as P

BF = jnp.bfloat16
F32 = jnp.float32
LOG2E = 1.4426950408889634

REQ = 16
NEW = 32
HD = 128
PAGES = 16
PAGE = 16
KEEP = PAGES * PAGE
NS = 16
RANK = 512
COLS = 640
CHUNK = 128
BC = 2 * NS
SUB = 16
STAT = 64
RET = 72
SEND = 96
TABLE = 6 * REQ
SHIFT = REQ.bit_length() - 1
TILES = RANK // HD
BLOCK = TILES * SUB + SUB // 2

VMEM = pl.BlockSpec(memory_space=pltpu.VMEM)
ANY = pl.BlockSpec(memory_space=pl.ANY)
HBM = pl.BlockSpec(memory_space=pltpu.HBM)
SMEM = pl.BlockSpec(memory_space=pltpu.SMEM)
SMALL = pltpu.CompilerParams(vmem_limit_bytes=12 * 1024 * 1024)
PARAMS = pltpu.CompilerParams(vmem_limit_bytes=60 * 1024 * 1024)


def tail_of(rest):
    lane = lax.broadcasted_iota(jnp.int32, rest.shape, 1)
    high = rest.astype(BF).astype(F32)
    low = pltpu.roll(rest - high, BC, 1)
    return jnp.where(lane < BC, high, jnp.where(lane < 2 * BC, low, 0.0))


def whole_tail(tail):
    return tail + pltpu.roll(tail, tail.shape[1] - BC, 1)


def store_block(ref, k, low, rest):
    for t in range(TILES):
        ref[k, t * SUB : (t + 1) * SUB, :] = low[:, t * HD : (t + 1) * HD].astype(BF)
    tail = tail_of(rest)
    both = tail[: SUB // 2] + pltpu.roll(tail[SUB // 2 :], HD // 2, 1)
    ref[k, TILES * SUB : BLOCK, :] = both.astype(BF)


def rest_of(both):
    return whole_tail(jnp.concatenate([both, pltpu.roll(both, HD // 2, 1)], axis=0))


def fetch(pairs, sems):
    copies = [pltpu.make_async_copy(a, b, sems.at[i]) for i, (a, b) in enumerate(pairs)]
    for copy in copies:
        copy.start()
    return copies


def pack_kernel(entries_hbm, q_hbm, cache_hbm, out_ref, tab, entries, q_ref, cache_ref, sems):
    copies = fetch([(entries_hbm, entries), (q_hbm, q_ref), (cache_hbm, cache_ref)], sems)
    me = lax.axis_index("req")
    for i in range(TABLE):
        tab[i] = 0
    copies[0].wait()
    for i in range(REQ):
        owner = entries[me * REQ + i] >> SHIFT
        count = tab[5 * REQ + owner]
        tab[jnp.minimum(count, 1) * REQ + owner] = i
        tab[5 * REQ + owner] = count + 1

    def one_peer(p, carry):
        first, last = jnp.int32(REQ - 1), jnp.int32(-1)
        for i in range(REQ):
            match = entries[p * REQ + i] >> SHIFT == me
            first = jnp.minimum(first, jnp.where(match, i, REQ - 1))
            last = jnp.where(match, i, last)
        tab[2 * REQ + p] = first
        tab[3 * REQ + p] = jnp.maximum(last, 0)
        tab[4 * REQ + p] = (last >= 0).astype(jnp.int32)
        return carry

    lax.fori_loop(0, REQ, one_peer, 0, unroll=2)
    copies[1].wait()
    copies[2].wait()
    for p in range(REQ):
        for k in range(2):
            slot = tab[k * REQ + p]
            out_ref[p, k * NEW : (k + 1) * NEW, :] = q_ref[
                pl.ds(pl.multiple_of(slot * NEW, NEW), NEW), :
            ]
            entry = entries[p * REQ + tab[(2 + k) * REQ + p]] & (REQ - 1)
            out_ref[p, 2 * NEW + k * NS : 2 * NEW + (k + 1) * NS, :] = cache_ref[entry].astype(BF)


def project_kernel(x_ref, w_ref, after, own_ref, *sent):
    at = lax.axis_index("mp")
    member = (at // (lax.axis_size("mp") // 2)) * 2 + (at & 1)
    for d in range(4):
        first = pl.multiple_of((member ^ d) * CHUNK, CHUNK)
        rows = x_ref[pl.ds(first, CHUNK), :]
        low = jnp.dot(rows, w_ref[:, :RANK], preferred_element_type=F32)
        rest = jnp.dot(rows, w_ref[:, RANK:], preferred_element_type=F32)
        rest = jnp.concatenate([rest, jnp.zeros((CHUNK, COLS - RANK - BC), F32)], axis=1)
        if d == 0:
            own_ref[:, :RANK] = low
            own_ref[:, RANK:] = rest
        else:
            for k in range(CHUNK // SUB):
                some = slice(k * SUB, (k + 1) * SUB)
                store_block(sent[d - 1], k, low[some], rest[some])


def add_four_kernel(own_ref, r1, r2, r3, after, out_ref):
    for k in range(CHUNK // SUB):
        some = slice(k * SUB, (k + 1) * SUB)
        block = r1[k].astype(F32) + r2[k].astype(F32) + r3[k].astype(F32)
        tiles = [block[t * SUB : (t + 1) * SUB] for t in range(TILES)]
        low = own_ref[some, :RANK] + jnp.concatenate(tiles, axis=1)
        store_block(out_ref, k, low, own_ref[some, RANK:] + rest_of(block[TILES * SUB :]))


def add_eight_kernel(parts, after, out_ref):
    block = parts[0].astype(F32)
    for k in range(1, CHUNK // SUB):
        block = block + parts[k].astype(F32)
    low = jnp.concatenate([block[t * SUB : (t + 1) * SUB] for t in range(TILES)], axis=1)
    rest = rest_of(block[TILES * SUB :])
    for k in range(CHUNK // SUB):
        store_block(out_ref, k, low, rest)


def gate_kernel(partial, after, out):
    pass


def heads_down(block):
    return jnp.concatenate([block[:, :HD], block[:, HD:]], axis=0)


def cached_kernel(tab, table, kept, got_ref, pool_ref, out_ref, done_ref):
    done_ref[...] = jnp.zeros(done_ref.shape, F32)
    row = lax.broadcasted_iota(jnp.int32, (2 * NEW, HD), 0)
    lane = lax.broadcasted_iota(jnp.int32, (2 * NEW, HD), 1)
    key = lax.broadcasted_iota(jnp.int32, (2 * NEW, KEEP), 1)
    base = lax.axis_index("req") * (REQ * PAGES)

    def one_peer(p, carry):
        @pl.when(tab[4 * REQ + p] > 0)
        def _():
            stats = []
            for k in range(2):
                slot = p * REQ + tab[(2 + k) * REQ + p]
                pages = [pool_ref[table[t * REQ * REQ + slot] - base] for t in range(PAGES)]
                rows = jnp.concatenate(pages, axis=0)
                q = heads_down(got_ref[p, k * NEW : (k + 1) * NEW, :])
                s = lax.dot_general(
                    q, rows[:, :HD], (((1,), (1,)), ((), ())), preferred_element_type=F32
                ) * (HD**-0.5)
                s = jnp.where(key < kept[slot], s, -1e30)
                top = jnp.max(s, axis=1, keepdims=True)
                w = jnp.exp(s - top)
                total = jnp.sum(w, axis=1, keepdims=True)
                o = jnp.dot(w.astype(BF), rows[:, HD:], preferred_element_type=F32) / total
                out_ref[p, k * NEW : (k + 1) * NEW, :] = jnp.concatenate(
                    [o[:NEW], o[NEW:]], axis=1
                ).astype(BF)
                lse = top + jnp.log(total)
                stats.append(jnp.sum(jnp.where(row == lane, lse, 0.0), axis=0, keepdims=True))
            flat = jnp.concatenate(stats, axis=0)
            hi = flat.astype(BF).astype(F32)
            mid = (flat - hi).astype(BF).astype(F32)
            low = flat - hi - mid
            none = jnp.zeros((6, HD), F32)
            left = jnp.concatenate([hi, low, none[:4]], axis=0)
            right = jnp.concatenate([mid, none], axis=0)
            out_ref[p, STAT:RET, :] = jnp.concatenate([left, right], axis=1).astype(BF)

        return carry

    lax.fori_loop(0, REQ, one_peer, 0)


def fresh_kernel(q_ref, kv_ref, out_ref, stat_ref):
    row = lax.broadcasted_iota(jnp.int32, (2 * NEW, HD), 0)
    lane = lax.broadcasted_iota(jnp.int32, (2 * NEW, HD), 1)
    query = lax.broadcasted_iota(jnp.int32, (2 * NEW, NEW), 0) & (NEW - 1)
    key = lax.broadcasted_iota(jnp.int32, (2 * NEW, NEW), 1)

    def one_slot(i, carry):
        first = pl.multiple_of(i * NEW, NEW)
        q = heads_down(q_ref[pl.ds(first, NEW), :])
        rows = kv_ref[pl.ds(first, NEW), :]
        s = lax.dot_general(
            q, rows[:, :HD], (((1,), (1,)), ((), ())), preferred_element_type=F32
        ) * (HD**-0.5)
        s = jnp.where(key <= query, s, -1e30)
        top = jnp.max(s, axis=1, keepdims=True)
        w = jnp.exp(s - top)
        total = jnp.sum(w, axis=1, keepdims=True)
        out_ref[i] = jnp.dot(w.astype(BF), rows[:, HD:], preferred_element_type=F32) / total
        lse = top + jnp.log(total)
        flat = jnp.sum(jnp.where(row == lane, lse, 0.0), axis=0, keepdims=True)
        stat_ref[i] = jnp.broadcast_to(flat, (8, HD))
        return carry

    lax.fori_loop(0, REQ, one_slot, 0, unroll=4)


def combine_kernel(tab, entries, fresh_len, part_ref, stat_ref, got_ref, after, out_ref):
    base = lax.axis_index("req") * REQ
    row = lax.broadcasted_iota(jnp.int32, (2 * NEW, HD), 0)
    lane = lax.broadcasted_iota(jnp.int32, (2 * NEW, HD), 1)
    spot = lax.broadcasted_iota(jnp.int32, (NEW, 2 * HD), 0)

    def one_slot(i, carry):
        first = pl.multiple_of(i * NEW, NEW)
        owner = entries[base + i] >> SHIFT
        second = (tab[REQ + owner] == i).astype(jnp.int32)
        old = heads_down(
            got_ref[owner, pl.ds(pl.multiple_of(second * NEW, NEW), NEW), :]
        ).astype(F32)
        stats = got_ref[owner, STAT:RET, :].astype(F32)
        exact = stats[0:2, :HD] + stats[0:2, HD:] + stats[2:4, :HD]
        lse_old = jnp.where(second > 0, exact[1:2], exact[0:1])
        lse = stat_ref[i, 0:1, :]
        most = jnp.maximum(lse_old, lse)
        weight_old = jnp.exp(lse_old - most)
        weight = jnp.exp(lse - most)
        share_old = weight_old / (weight_old + weight)
        share_old = jnp.sum(jnp.where(row == lane, share_old, 0.0), axis=1, keepdims=True)
        share = weight / (weight_old + weight)
        share = jnp.sum(jnp.where(row == lane, share, 0.0), axis=1, keepdims=True)
        o = old * share_old + part_ref[i] * share
        o = jnp.concatenate([o[:NEW], o[NEW:]], axis=1)
        live = spot < fresh_len[base + i]
        out_ref[pl.ds(first, NEW), :] = jnp.where(live, o, 0.0).astype(BF)
        return carry

    lax.fori_loop(0, REQ, one_slot, 0, unroll=4)


def scan_kernel(
    tab, entries, fresh_len, low_ref, wdt_hbm, b_ref, a_ref, d_ref, x_hbm, g_hbm, got_hbm,
    out_ref, state_ref, done_ref, dt_s, u_s, bc_s, y_s, a_s, h_s, wdt_ref, x_ref, g_ref, got_ref, sems,
):
    copies = fetch(
        [(wdt_hbm, wdt_ref), (x_hbm, x_ref), (got_hbm, got_ref), (g_hbm, g_ref)], sems
    )
    done_ref[...] = jnp.zeros(done_ref.shape, F32)
    base = lax.axis_index("req") * REQ
    channels = x_ref.shape[1]
    halves = [slice(c * HD, (c + 1) * HD) for c in range(channels // HD)]
    step = lax.broadcasted_iota(jnp.int32, (NEW, channels), 0)
    for n in range(NS):
        a_s[n * 8 : (n + 1) * 8, :] = jnp.broadcast_to(a_ref[n : n + 1, :] * (-LOG2E), (8, channels))
    copies[0].wait()
    copies[1].wait()
    for member in range(4):
        first = member * CHUNK
        low = []
        for k in range(CHUNK // SUB):
            at = member * (CHUNK // SUB) + k
            tiles = [low_ref[at, t * SUB : (t + 1) * SUB, :] for t in range(TILES)]
            low.append(jnp.concatenate(tiles, axis=1))
            bc_s[first + k * SUB : first + (k + 1) * SUB, :] = rest_of(
                low_ref[at, TILES * SUB : BLOCK, :].astype(F32)
            )
        low = jnp.concatenate(low, axis=0)
        pre = jnp.dot(low, wdt_ref[...], preferred_element_type=F32) + b_ref[...]
        dt = jnp.maximum(pre, 0.0) + jnp.log1p(jnp.exp(-jnp.abs(pre)))
        for j in range(CHUNK // NEW):
            here = first + j * NEW
            live = step < fresh_len[base + member * (CHUNK // NEW) + j]
            masked = jnp.where(live, dt[j * NEW : (j + 1) * NEW], 0.0)
            drive = masked * x_ref[pl.ds(here, NEW), :].astype(F32)
            for c, half in enumerate(halves):
                dt_s[c, pl.ds(here, NEW), :] = masked[:, half]
                u_s[c, pl.ds(here, NEW), :] = drive[:, half]
    copies[2].wait()
    for i in range(REQ):
        owner = entries[base + i] >> SHIFT
        second = (tab[REQ + owner] == i).astype(jnp.int32)
        start = pl.multiple_of(2 * NEW + second * NS, NS)
        state = got_ref[owner, pl.ds(start, NS), :].astype(F32)
        for c, half in enumerate(halves):
            h_s[c, i * NS : (i + 1) * NS, :] = state[:, half]
    for g in range(2):
        begin = g * 8 * NS
        h0 = tuple(
            tuple(h_s[c, pl.ds(begin + n, 8, stride=NS), :] for c in range(len(halves)))
            for n in range(NS)
        )

        def one_step(i, hs):
            rows = pl.ds(g * 8 * NEW + i, 8, stride=NEW)
            dt = [dt_s[c, rows, :] for c in range(len(halves))]
            u = [u_s[c, rows, :] for c in range(len(halves))]
            bc = bc_s[rows, :]
            y = [0.0] * len(halves)
            new = []
            for n in range(NS):
                b_in = jnp.broadcast_to(bc[:, n : n + 1], (8, HD))
                c_out = jnp.broadcast_to(bc[:, NS + n : NS + n + 1], (8, HD))
                pair = []
                for c, half in enumerate(halves):
                    decay = jnp.exp2(dt[c] * a_s[n * 8 : (n + 1) * 8, half])
                    h = decay * hs[n][c] + u[c] * b_in
                    y[c] = y[c] + h * c_out
                    pair.append(h)
                new.append(tuple(pair))
            for c in range(len(halves)):
                y_s[c, rows, :] = y[c]
            return tuple(new)

        hs = lax.fori_loop(0, NEW, one_step, h0, unroll=8)
        for n in range(NS):
            for c in range(len(halves)):
                h_s[c, pl.ds(begin + n, 8, stride=NS), :] = hs[n][c]
    for c, half in enumerate(halves):
        state_ref[:, half] = h_s[c]
    copies[3].wait()
    for i in range(REQ):
        rows = slice(i * NEW, (i + 1) * NEW)
        for c, half in enumerate(halves):
            gate = g_ref[rows, half].astype(F32)
            y = y_s[c, rows, :] + d_ref[:, half] * x_ref[rows, half].astype(F32)
            y = y * (gate * jax.nn.sigmoid(gate))
            out_ref[rows, half] = jnp.where(step[:, half] < fresh_len[base + i], y, 0.0).astype(BF)


def on_device(
    queries, kv_new, kv_pool, ssm_cache, mixer_in, gate_in, w_x, w_dt, b_dt, a_rate, d_skip,
    kept_len, new_len, cache_index, page_table,
):
    rows, channels = mixer_in.shape
    zs = lax.axis_size("mp") // 2

    packed, tab = pl.pallas_call(
        pack_kernel,
        out_shape=[
            jax.ShapeDtypeStruct((REQ, SEND, channels), BF),
            jax.ShapeDtypeStruct((TABLE,), jnp.int32),
        ],
        in_specs=[HBM, HBM, HBM],
        out_specs=[VMEM, SMEM],
        scratch_shapes=[
            pltpu.SMEM(cache_index.shape, jnp.int32),
            pltpu.VMEM(queries.shape, BF),
            pltpu.VMEM(ssm_cache.shape, F32),
            pltpu.SemaphoreType.DMA((3,)),
        ],
        compiler_params=PARAMS,
        name="pack",
    )(cache_index, queries, ssm_cache)
    got = lax.all_to_all(packed, "req", 0, 0, tiled=True)

    chunk = jax.ShapeDtypeStruct((CHUNK // SUB, BLOCK, HD), BF)
    own, *sent = pl.pallas_call(
        project_kernel,
        out_shape=[jax.ShapeDtypeStruct((CHUNK, COLS), F32), chunk, chunk, chunk],
        in_specs=[VMEM, VMEM, ANY],
        out_specs=[VMEM] * 4,
        compiler_params=SMALL,
        name="project",
    )(mixer_in, w_x, packed)

    def swap(array, d):
        pairs = []
        for i in range(2 * zs):
            y, z = i // zs, i % zs
            pairs.append((i, (y ^ (d >> 1)) * zs + (z ^ (d & 1))))
        return lax.ppermute(array, "mp", pairs)

    quads = [[y * zs + 2 * k + b for y in range(2) for b in range(2)] for k in range(zs // 2)]
    groups = [[y * zs + 2 * k + b for k in range(zs // 2)] for y in range(2) for b in range(2)]
    received = [swap(sent[d - 1], d) for d in (1, 2, 3)]
    block = jax.ShapeDtypeStruct((REQ, 2 * NEW, HD), F32)
    fresh = pl.pallas_call(
        fresh_kernel,
        out_shape=[block, jax.ShapeDtypeStruct((REQ, 8, HD), F32)],
        in_specs=[VMEM] * 2,
        out_specs=[VMEM] * 2,
        compiler_params=SMALL,
        name="fresh",
    )(queries, kv_new.reshape(rows, channels))
    added = pl.pallas_call(
        add_four_kernel,
        out_shape=chunk,
        in_specs=[VMEM] * 4 + [ANY],
        out_specs=VMEM,
        compiler_params=SMALL,
        name="add_four",
    )(own, *received, fresh[1])
    token = jax.ShapeDtypeStruct((8, HD), F32)
    partial, cached = pl.pallas_call(
        cached_kernel,
        out_shape=[jax.ShapeDtypeStruct((REQ, RET, channels), BF), token],
        in_specs=[SMEM, SMEM, SMEM, VMEM, VMEM],
        out_specs=[VMEM] * 2,
        compiler_params=SMALL,
        name="cached",
    )(tab, page_table.T.reshape(-1), kept_len, got, kv_pool.reshape(-1, PAGE, channels))
    parts = lax.all_to_all(added, "mp", 0, 0, tiled=True, axis_index_groups=groups)
    summed = pl.pallas_call(
        add_eight_kernel,
        out_shape=chunk,
        in_specs=[VMEM, ANY],
        out_specs=VMEM,
        compiler_params=SMALL,
        name="add_eight",
    )(parts, cached)
    whole = lax.all_to_all(summed, "mp", 0, 0, tiled=True, axis_index_groups=groups)
    whole = jnp.concatenate([whole] * 4, axis=0)
    whole = lax.all_to_all(whole, "mp", 0, 0, tiled=True, axis_index_groups=quads)

    partial = pl.pallas_call(
        gate_kernel,
        out_shape=jax.ShapeDtypeStruct(partial.shape, BF),
        in_specs=[ANY] * 2,
        out_specs=ANY,
        input_output_aliases={0: 0},
        compiler_params=PARAMS,
        name="gate",
    )(partial, whole)
    back = lax.all_to_all(partial, "req", 0, 0, tiled=True)

    mixer_out, state_out, done = pl.pallas_call(
        scan_kernel,
        out_shape=[
            jax.ShapeDtypeStruct((rows, channels), BF),
            jax.ShapeDtypeStruct((REQ * NS, channels), F32),
            token,
        ],
        in_specs=[SMEM] * 3 + [VMEM, HBM] + [VMEM] * 3 + [HBM] * 3,
        out_specs=[VMEM] * 3,
        scratch_shapes=[
            pltpu.VMEM((channels // HD, rows, HD), F32),
            pltpu.VMEM((channels // HD, rows, HD), F32),
            pltpu.VMEM((rows, COLS - RANK), F32),
            pltpu.VMEM((channels // HD, rows, HD), F32),
            pltpu.VMEM((NS * 8, channels), F32),
            pltpu.VMEM((channels // HD, REQ * NS, HD), F32),
            pltpu.VMEM(w_dt.shape, BF),
            pltpu.VMEM((rows, channels), BF),
            pltpu.VMEM((rows, channels), BF),
            pltpu.VMEM(got.shape, BF),
            pltpu.SemaphoreType.DMA((4,)),
        ],
        compiler_params=PARAMS,
        name="scan",
    )(
        tab, cache_index, new_len, whole, w_dt, b_dt.reshape(1, -1), a_rate,
        d_skip.reshape(1, -1), mixer_in, gate_in, got,
    )
    attn_out = pl.pallas_call(
        combine_kernel,
        out_shape=jax.ShapeDtypeStruct((rows, channels), BF),
        in_specs=[SMEM] * 3 + [VMEM] * 3 + [ANY],
        out_specs=VMEM,
        compiler_params=SMALL,
        name="combine",
    )(tab, cache_index, new_len, *fresh, back, done)
    return attn_out, mixer_out, state_out.reshape(REQ, NS, channels)


def solution(mesh):
    placed = (
        P("req", "mp"),
        P("req", "mp", None),
        P("req", None, "mp", None),
        P("req", None, "mp"),
        P("req", "mp"),
        P("req", "mp"),
        P("mp", None),
        P(None, "mp"),
        P("mp"),
        P(None, "mp"),
        P("mp"),
        P(),
        P(),
        P(),
        P(),
    )
    return jax.shard_map(
        on_device,
        mesh=mesh,
        in_specs=placed,
        out_specs=(P("req", "mp"), P("req", "mp"), P("req", None, "mp")),
        check_vma=False,
    )
```

```python
import functools

import jax
import jax.numpy as jnp
from jax import lax
from jax.experimental import pallas as pl
from jax.experimental.pallas import tpu as pltpu
from jax.sharding import PartitionSpec as P

BF = jnp.bfloat16
F32 = jnp.float32
LOG2E = 1.4426950408889634

REQ = 16
NEW = 32
HD = 128
PAGES = 16
PAGE = 16
KEEP = PAGES * PAGE
NS = 16
RANK = 512
COLS = 640
CHUNK = 128
BC = 2 * NS
SUB = 16
STAT = 64
RET = 72
SEND = 96
TABLE = 6 * REQ
SHIFT = REQ.bit_length() - 1
TILES = RANK // HD
BLOCK = TILES * SUB + SUB // 2

VMEM = pl.BlockSpec(memory_space=pltpu.VMEM)
ANY = pl.BlockSpec(memory_space=pl.ANY)
HBM = pl.BlockSpec(memory_space=pltpu.HBM)
SMEM = pl.BlockSpec(memory_space=pltpu.SMEM)
SMALL = pltpu.CompilerParams(vmem_limit_bytes=12 * 1024 * 1024)
MIDDLE = pltpu.CompilerParams(vmem_limit_bytes=32 * 1024 * 1024)
PARAMS = pltpu.CompilerParams(vmem_limit_bytes=60 * 1024 * 1024)


def tail_of(rest):
    lane = lax.broadcasted_iota(jnp.int32, rest.shape, 1)
    high = rest.astype(BF).astype(F32)
    low = pltpu.roll(rest - high, BC, 1)
    return jnp.where(lane < BC, high, jnp.where(lane < 2 * BC, low, 0.0))


def whole_tail(tail):
    return tail + pltpu.roll(tail, tail.shape[1] - BC, 1)


def store_block(ref, k, low, rest):
    for t in range(TILES):
        ref[k, t * SUB : (t + 1) * SUB, :] = low[:, t * HD : (t + 1) * HD].astype(BF)
    tail = tail_of(rest)
    both = tail[: SUB // 2] + pltpu.roll(tail[SUB // 2 :], HD // 2, 1)
    ref[k, TILES * SUB : BLOCK, :] = both.astype(BF)


def rest_of(both):
    return whole_tail(jnp.concatenate([both, pltpu.roll(both, HD // 2, 1)], axis=0))


def fetch(pairs, sems):
    copies = [pltpu.make_async_copy(a, b, sems.at[i]) for i, (a, b) in enumerate(pairs)]
    for copy in copies:
        copy.start()
    return copies


def pack_kernel(entries_hbm, q_hbm, cache_hbm, out_ref, tab, entries, q_ref, cache_ref, sems):
    copies = fetch([(entries_hbm, entries), (q_hbm, q_ref), (cache_hbm, cache_ref)], sems)
    me = lax.axis_index("req")
    for i in range(TABLE):
        tab[i] = 0
    copies[0].wait()
    for i in range(REQ):
        owner = entries[me * REQ + i] >> SHIFT
        count = tab[5 * REQ + owner]
        tab[jnp.minimum(count, 1) * REQ + owner] = i
        tab[5 * REQ + owner] = count + 1

    def one_peer(p, carry):
        first, last = jnp.int32(REQ - 1), jnp.int32(-1)
        for i in range(REQ):
            match = entries[p * REQ + i] >> SHIFT == me
            first = jnp.minimum(first, jnp.where(match, i, REQ - 1))
            last = jnp.where(match, i, last)
        tab[2 * REQ + p] = first
        tab[3 * REQ + p] = jnp.maximum(last, 0)
        tab[4 * REQ + p] = (last >= 0).astype(jnp.int32)
        return carry

    lax.fori_loop(0, REQ, one_peer, 0, unroll=2)
    copies[1].wait()
    copies[2].wait()
    for p in range(REQ):
        for k in range(2):
            slot = tab[k * REQ + p]
            out_ref[p, k * NEW : (k + 1) * NEW, :] = q_ref[
                pl.ds(pl.multiple_of(slot * NEW, NEW), NEW), :
            ]
            entry = entries[p * REQ + tab[(2 + k) * REQ + p]] & (REQ - 1)
            out_ref[p, 2 * NEW + k * NS : 2 * NEW + (k + 1) * NS, :] = cache_ref[entry].astype(BF)


def project_kernel(x_ref, w_ref, after, own_ref, *sent):
    at = lax.axis_index("mp")
    member = (at // (lax.axis_size("mp") // 2)) * 2 + (at & 1)
    for d in range(4):
        first = pl.multiple_of((member ^ d) * CHUNK, CHUNK)
        rows = x_ref[pl.ds(first, CHUNK), :]
        low = jnp.dot(rows, w_ref[:, :RANK], preferred_element_type=F32)
        rest = jnp.dot(rows, w_ref[:, RANK:], preferred_element_type=F32)
        rest = jnp.concatenate([rest, jnp.zeros((CHUNK, COLS - RANK - BC), F32)], axis=1)
        if d == 0:
            own_ref[:, :RANK] = low
            own_ref[:, RANK:] = rest
        else:
            for k in range(CHUNK // SUB):
                some = slice(k * SUB, (k + 1) * SUB)
                store_block(sent[d - 1], k, low[some], rest[some])


def add_four_kernel(own_ref, r1, r2, r3, after, out_ref):
    for k in range(CHUNK // SUB):
        some = slice(k * SUB, (k + 1) * SUB)
        block = r1[k].astype(F32) + r2[k].astype(F32) + r3[k].astype(F32)
        tiles = [block[t * SUB : (t + 1) * SUB] for t in range(TILES)]
        low = own_ref[some, :RANK] + jnp.concatenate(tiles, axis=1)
        store_block(out_ref, k, low, own_ref[some, RANK:] + rest_of(block[TILES * SUB :]))


def add_eight_kernel(parts, after, out_ref):
    block = parts[0].astype(F32)
    for k in range(1, CHUNK // SUB):
        block = block + parts[k].astype(F32)
    low = jnp.concatenate([block[t * SUB : (t + 1) * SUB] for t in range(TILES)], axis=1)
    rest = rest_of(block[TILES * SUB :])
    for k in range(CHUNK // SUB):
        store_block(out_ref, k, low, rest)


def gate_kernel(partial, after, out):
    pass


def heads_down(block):
    return jnp.concatenate([block[:, :HD], block[:, HD:]], axis=0)


def cached_kernel(tab, table, kept, got_ref, pool_ref, out_ref, done_ref):
    done_ref[...] = jnp.zeros(done_ref.shape, F32)
    row = lax.broadcasted_iota(jnp.int32, (2 * NEW, HD), 0)
    lane = lax.broadcasted_iota(jnp.int32, (2 * NEW, HD), 1)
    key = lax.broadcasted_iota(jnp.int32, (2 * NEW, KEEP), 1)
    base = lax.axis_index("req") * (REQ * PAGES)

    def one_peer(p, carry):
        @pl.when(tab[4 * REQ + p] > 0)
        def _():
            stats = []
            for k in range(2):
                slot = p * REQ + tab[(2 + k) * REQ + p]
                pages = [pool_ref[table[t * REQ * REQ + slot] - base] for t in range(PAGES)]
                rows = jnp.concatenate(pages, axis=0)
                q = heads_down(got_ref[p, k * NEW : (k + 1) * NEW, :])
                s = lax.dot_general(
                    q, rows[:, :HD], (((1,), (1,)), ((), ())), preferred_element_type=F32
                ) * (HD**-0.5)
                s = jnp.where(key < kept[slot], s, -1e30)
                top = jnp.max(s, axis=1, keepdims=True)
                w = jnp.exp(s - top)
                total = jnp.sum(w, axis=1, keepdims=True)
                o = jnp.dot(w.astype(BF), rows[:, HD:], preferred_element_type=F32) / total
                out_ref[p, k * NEW : (k + 1) * NEW, :] = jnp.concatenate(
                    [o[:NEW], o[NEW:]], axis=1
                ).astype(BF)
                lse = top + jnp.log(total)
                stats.append(jnp.sum(jnp.where(row == lane, lse, 0.0), axis=0, keepdims=True))
            flat = jnp.concatenate(stats, axis=0)
            hi = flat.astype(BF).astype(F32)
            mid = (flat - hi).astype(BF).astype(F32)
            low = flat - hi - mid
            none = jnp.zeros((6, HD), F32)
            left = jnp.concatenate([hi, low, none[:4]], axis=0)
            right = jnp.concatenate([mid, none], axis=0)
            out_ref[p, STAT:RET, :] = jnp.concatenate([left, right], axis=1).astype(BF)

        return carry

    lax.fori_loop(0, REQ, one_peer, 0)


def fresh_kernel(q_ref, kv_ref, out_ref, stat_ref):
    row = lax.broadcasted_iota(jnp.int32, (2 * NEW, HD), 0)
    lane = lax.broadcasted_iota(jnp.int32, (2 * NEW, HD), 1)
    query = lax.broadcasted_iota(jnp.int32, (2 * NEW, NEW), 0) & (NEW - 1)
    key = lax.broadcasted_iota(jnp.int32, (2 * NEW, NEW), 1)

    def one_slot(i, carry):
        first = pl.multiple_of(i * NEW, NEW)
        q = heads_down(q_ref[pl.ds(first, NEW), :])
        rows = kv_ref[pl.ds(first, NEW), :]
        s = lax.dot_general(
            q, rows[:, :HD], (((1,), (1,)), ((), ())), preferred_element_type=F32
        ) * (HD**-0.5)
        s = jnp.where(key <= query, s, -1e30)
        top = jnp.max(s, axis=1, keepdims=True)
        w = jnp.exp(s - top)
        total = jnp.sum(w, axis=1, keepdims=True)
        out_ref[i] = jnp.dot(w.astype(BF), rows[:, HD:], preferred_element_type=F32) / total
        lse = top + jnp.log(total)
        flat = jnp.sum(jnp.where(row == lane, lse, 0.0), axis=0, keepdims=True)
        stat_ref[i] = jnp.broadcast_to(flat, (8, HD))
        return carry

    lax.fori_loop(0, REQ, one_slot, 0, unroll=4)


def combine_kernel(tab, entries, fresh_len, part_ref, stat_ref, got_ref, after, out_ref):
    base = lax.axis_index("req") * REQ
    row = lax.broadcasted_iota(jnp.int32, (2 * NEW, HD), 0)
    lane = lax.broadcasted_iota(jnp.int32, (2 * NEW, HD), 1)
    spot = lax.broadcasted_iota(jnp.int32, (NEW, 2 * HD), 0)

    def one_slot(i, carry):
        first = pl.multiple_of(i * NEW, NEW)
        owner = entries[base + i] >> SHIFT
        second = (tab[REQ + owner] == i).astype(jnp.int32)
        old = heads_down(
            got_ref[owner, pl.ds(pl.multiple_of(second * NEW, NEW), NEW), :]
        ).astype(F32)
        stats = got_ref[owner, STAT:RET, :].astype(F32)
        exact = stats[0:2, :HD] + stats[0:2, HD:] + stats[2:4, :HD]
        lse_old = jnp.where(second > 0, exact[1:2], exact[0:1])
        lse = stat_ref[i, 0:1, :]
        most = jnp.maximum(lse_old, lse)
        weight_old = jnp.exp(lse_old - most)
        weight = jnp.exp(lse - most)
        share_old = weight_old / (weight_old + weight)
        share_old = jnp.sum(jnp.where(row == lane, share_old, 0.0), axis=1, keepdims=True)
        share = weight / (weight_old + weight)
        share = jnp.sum(jnp.where(row == lane, share, 0.0), axis=1, keepdims=True)
        o = old * share_old + part_ref[i] * share
        o = jnp.concatenate([o[:NEW], o[NEW:]], axis=1)
        live = spot < fresh_len[base + i]
        out_ref[pl.ds(first, NEW), :] = jnp.where(live, o, 0.0).astype(BF)
        return carry

    lax.fori_loop(0, REQ, one_slot, 0, unroll=4)


def scan_kernel(
    tab, entries, fresh_len, low_ref, wdt_hbm, b_ref, a_ref, d_ref, x_hbm, g_hbm, got_hbm,
    out_ref, state_ref, done_ref, dt_s, u_s, bc_s, y_s, a_s, h_s, wdt_ref, x_ref, g_ref, got_ref, sems,
):
    copies = fetch(
        [(wdt_hbm, wdt_ref), (x_hbm, x_ref), (got_hbm, got_ref), (g_hbm, g_ref)], sems
    )
    done_ref[...] = jnp.zeros(done_ref.shape, F32)
    base = lax.axis_index("req") * REQ
    channels = x_ref.shape[1]
    halves = [slice(c * HD, (c + 1) * HD) for c in range(channels // HD)]
    step = lax.broadcasted_iota(jnp.int32, (NEW, channels), 0)
    for n in range(NS):
        a_s[n * 8 : (n + 1) * 8, :] = jnp.broadcast_to(a_ref[n : n + 1, :] * (-LOG2E), (8, channels))
    for at in range(low_ref.shape[0]):
        bc_s[at * SUB : (at + 1) * SUB, :] = rest_of(low_ref[at, TILES * SUB : BLOCK, :].astype(F32))
    copies[0].wait()
    copies[1].wait()
    for member in range(4):
        first = member * CHUNK
        low = []
        for k in range(CHUNK // SUB):
            at = member * (CHUNK // SUB) + k
            tiles = [low_ref[at, t * SUB : (t + 1) * SUB, :] for t in range(TILES)]
            low.append(jnp.concatenate(tiles, axis=1))
        low = jnp.concatenate(low, axis=0)
        pre = jnp.dot(low, wdt_ref[...], preferred_element_type=F32) + b_ref[...]
        dt = jnp.maximum(pre, 0.0) + jnp.log1p(jnp.exp(-jnp.abs(pre)))
        for j in range(CHUNK // NEW):
            here = first + j * NEW
            live = step < fresh_len[base + member * (CHUNK // NEW) + j]
            masked = jnp.where(live, dt[j * NEW : (j + 1) * NEW], 0.0)
            drive = masked * x_ref[pl.ds(here, NEW), :].astype(F32)
            for c, half in enumerate(halves):
                dt_s[c, pl.ds(here, NEW), :] = masked[:, half]
                u_s[c, pl.ds(here, NEW), :] = drive[:, half]
    copies[2].wait()
    for i in range(REQ):
        owner = entries[base + i] >> SHIFT
        second = (tab[REQ + owner] == i).astype(jnp.int32)
        start = pl.multiple_of(2 * NEW + second * NS, NS)
        state = got_ref[owner, pl.ds(start, NS), :].astype(F32)
        for c, half in enumerate(halves):
            h_s[c, i * NS : (i + 1) * NS, :] = state[:, half]
    for g in range(2):
        begin = g * 8 * NS
        h0 = tuple(
            tuple(h_s[c, pl.ds(begin + n, 8, stride=NS), :] for c in range(len(halves)))
            for n in range(NS)
        )

        def one_step(i, hs):
            rows = pl.ds(g * 8 * NEW + i, 8, stride=NEW)
            dt = [dt_s[c, rows, :] for c in range(len(halves))]
            u = [u_s[c, rows, :] for c in range(len(halves))]
            bc = bc_s[rows, :]
            y = [0.0] * len(halves)
            new = []
            for n in range(NS):
                b_in = jnp.broadcast_to(bc[:, n : n + 1], (8, HD))
                c_out = jnp.broadcast_to(bc[:, NS + n : NS + n + 1], (8, HD))
                pair = []
                for c, half in enumerate(halves):
                    decay = jnp.exp2(dt[c] * a_s[n * 8 : (n + 1) * 8, half])
                    h = decay * hs[n][c] + u[c] * b_in
                    y[c] = y[c] + h * c_out
                    pair.append(h)
                new.append(tuple(pair))
            for c in range(len(halves)):
                y_s[c, rows, :] = y[c]
            return tuple(new)

        hs = lax.fori_loop(0, NEW, one_step, h0, unroll=16)
        for n in range(NS):
            for c in range(len(halves)):
                h_s[c, pl.ds(begin + n, 8, stride=NS), :] = hs[n][c]
    for c, half in enumerate(halves):
        state_ref[:, half] = h_s[c]
    copies[3].wait()
    for i in range(REQ):
        rows = slice(i * NEW, (i + 1) * NEW)
        for c, half in enumerate(halves):
            gate = g_ref[rows, half].astype(F32)
            y = y_s[c, rows, :] + d_ref[:, half] * x_ref[rows, half].astype(F32)
            y = y * (gate * jax.nn.sigmoid(gate))
            out_ref[rows, half] = jnp.where(step[:, half] < fresh_len[base + i], y, 0.0).astype(BF)


def on_device(
    queries, kv_new, kv_pool, ssm_cache, mixer_in, gate_in, w_x, w_dt, b_dt, a_rate, d_skip,
    kept_len, new_len, cache_index, page_table,
):
    rows, channels = mixer_in.shape
    zs = lax.axis_size("mp") // 2

    packed, tab = pl.pallas_call(
        pack_kernel,
        out_shape=[
            jax.ShapeDtypeStruct((REQ, SEND, channels), BF),
            jax.ShapeDtypeStruct((TABLE,), jnp.int32),
        ],
        in_specs=[HBM, HBM, HBM],
        out_specs=[VMEM, SMEM],
        scratch_shapes=[
            pltpu.SMEM(cache_index.shape, jnp.int32),
            pltpu.VMEM(queries.shape, BF),
            pltpu.VMEM(ssm_cache.shape, F32),
            pltpu.SemaphoreType.DMA((3,)),
        ],
        compiler_params=PARAMS,
        name="pack",
    )(cache_index, queries, ssm_cache)
    got = lax.all_to_all(packed, "req", 0, 0, tiled=True)

    chunk = jax.ShapeDtypeStruct((CHUNK // SUB, BLOCK, HD), BF)
    own, *sent = pl.pallas_call(
        project_kernel,
        out_shape=[jax.ShapeDtypeStruct((CHUNK, COLS), F32), chunk, chunk, chunk],
        in_specs=[VMEM, VMEM, ANY],
        out_specs=[VMEM] * 4,
        compiler_params=SMALL,
        name="project",
    )(mixer_in, w_x, packed)

    def swap(array, d):
        pairs = []
        for i in range(2 * zs):
            y, z = i // zs, i % zs
            pairs.append((i, (y ^ (d >> 1)) * zs + (z ^ (d & 1))))
        return lax.ppermute(array, "mp", pairs)

    quads = [[y * zs + 2 * k + b for y in range(2) for b in range(2)] for k in range(zs // 2)]
    groups = [[y * zs + 2 * k + b for k in range(zs // 2)] for y in range(2) for b in range(2)]
    received = [swap(sent[d - 1], d) for d in (1, 2, 3)]
    block = jax.ShapeDtypeStruct((REQ, 2 * NEW, HD), F32)
    fresh = pl.pallas_call(
        fresh_kernel,
        out_shape=[block, jax.ShapeDtypeStruct((REQ, 8, HD), F32)],
        in_specs=[VMEM] * 2,
        out_specs=[VMEM] * 2,
        compiler_params=SMALL,
        name="fresh",
    )(queries, kv_new.reshape(rows, channels))
    added = pl.pallas_call(
        add_four_kernel,
        out_shape=chunk,
        in_specs=[VMEM] * 4 + [ANY],
        out_specs=VMEM,
        compiler_params=SMALL,
        name="add_four",
    )(own, *received, fresh[1])
    token = jax.ShapeDtypeStruct((8, HD), F32)
    partial, cached = pl.pallas_call(
        cached_kernel,
        out_shape=[jax.ShapeDtypeStruct((REQ, RET, channels), BF), token],
        in_specs=[SMEM, SMEM, SMEM, VMEM, VMEM],
        out_specs=[VMEM] * 2,
        compiler_params=SMALL,
        name="cached",
    )(tab, page_table.T.reshape(-1), kept_len, got, kv_pool.reshape(-1, PAGE, channels))
    parts = lax.all_to_all(added, "mp", 0, 0, tiled=True, axis_index_groups=groups)
    summed = pl.pallas_call(
        add_eight_kernel,
        out_shape=chunk,
        in_specs=[VMEM, ANY],
        out_specs=VMEM,
        compiler_params=SMALL,
        name="add_eight",
    )(parts, cached)
    whole = lax.all_to_all(summed, "mp", 0, 0, tiled=True, axis_index_groups=groups)
    whole = jnp.concatenate([whole] * 4, axis=0)
    whole = lax.all_to_all(whole, "mp", 0, 0, tiled=True, axis_index_groups=quads)

    partial = pl.pallas_call(
        gate_kernel,
        out_shape=jax.ShapeDtypeStruct(partial.shape, BF),
        in_specs=[ANY] * 2,
        out_specs=ANY,
        input_output_aliases={0: 0},
        compiler_params=PARAMS,
        name="gate",
    )(partial, whole)
    back = lax.all_to_all(partial, "req", 0, 0, tiled=True)

    mixer_out, state_out, done = pl.pallas_call(
        scan_kernel,
        out_shape=[
            jax.ShapeDtypeStruct((rows, channels), BF),
            jax.ShapeDtypeStruct((REQ * NS, channels), F32),
            token,
        ],
        in_specs=[SMEM] * 3 + [VMEM, HBM] + [VMEM] * 3 + [HBM] * 3,
        out_specs=[VMEM] * 3,
        scratch_shapes=[
            pltpu.VMEM((channels // HD, rows, HD), F32),
            pltpu.VMEM((channels // HD, rows, HD), F32),
            pltpu.VMEM((rows, COLS - RANK), F32),
            pltpu.VMEM((channels // HD, rows, HD), F32),
            pltpu.VMEM((NS * 8, channels), F32),
            pltpu.VMEM((channels // HD, REQ * NS, HD), F32),
            pltpu.VMEM(w_dt.shape, BF),
            pltpu.VMEM((rows, channels), BF),
            pltpu.VMEM((rows, channels), BF),
            pltpu.VMEM(got.shape, BF),
            pltpu.SemaphoreType.DMA((4,)),
        ],
        compiler_params=MIDDLE,
        name="scan",
    )(
        tab, cache_index, new_len, whole, w_dt, b_dt.reshape(1, -1), a_rate,
        d_skip.reshape(1, -1), mixer_in, gate_in, got,
    )
    attn_out = pl.pallas_call(
        combine_kernel,
        out_shape=jax.ShapeDtypeStruct((rows, channels), BF),
        in_specs=[SMEM] * 3 + [VMEM] * 3 + [ANY],
        out_specs=VMEM,
        compiler_params=SMALL,
        name="combine",
    )(tab, cache_index, new_len, *fresh, back, done)
    return attn_out, mixer_out, state_out.reshape(REQ, NS, channels)


def solution(mesh):
    placed = (
        P("req", "mp"),
        P("req", "mp", None),
        P("req", None, "mp", None),
        P("req", None, "mp"),
        P("req", "mp"),
        P("req", "mp"),
        P("mp", None),
        P(None, "mp"),
        P("mp"),
        P(None, "mp"),
        P("mp"),
        P(),
        P(),
        P(),
        P(),
    )
    return jax.shard_map(
        on_device,
        mesh=mesh,
        in_specs=placed,
        out_specs=(P("req", "mp"), P("req", "mp"), P("req", None, "mp")),
        check_vma=False,
    )
```

```python
import functools

import jax
import jax.numpy as jnp
from jax import lax
from jax.experimental import pallas as pl
from jax.experimental.pallas import tpu as pltpu
from jax.sharding import PartitionSpec as P

BF = jnp.bfloat16
F32 = jnp.float32
LOG2E = 1.4426950408889634

REQ = 16
NEW = 32
HD = 128
PAGES = 16
PAGE = 16
KEEP = PAGES * PAGE
NS = 16
RANK = 512
COLS = 640
CHUNK = 128
BC = 2 * NS
SUB = 16
STAT = 64
RET = 72
SEND = 96
TABLE = 6 * REQ
SHIFT = REQ.bit_length() - 1
TILES = RANK // HD
BLOCK = TILES * SUB + SUB // 2

VMEM = pl.BlockSpec(memory_space=pltpu.VMEM)
ANY = pl.BlockSpec(memory_space=pl.ANY)
HBM = pl.BlockSpec(memory_space=pltpu.HBM)
SMEM = pl.BlockSpec(memory_space=pltpu.SMEM)
SMALL = pltpu.CompilerParams(vmem_limit_bytes=12 * 1024 * 1024)
MIDDLE = pltpu.CompilerParams(vmem_limit_bytes=32 * 1024 * 1024)
PARAMS = pltpu.CompilerParams(vmem_limit_bytes=60 * 1024 * 1024)


def tail_of(rest):
    lane = lax.broadcasted_iota(jnp.int32, rest.shape, 1)
    high = rest.astype(BF).astype(F32)
    low = pltpu.roll(rest - high, BC, 1)
    return jnp.where(lane < BC, high, jnp.where(lane < 2 * BC, low, 0.0))


def whole_tail(tail):
    return tail + pltpu.roll(tail, tail.shape[1] - BC, 1)


def store_block(ref, k, low, rest):
    for t in range(TILES):
        ref[k, t * SUB : (t + 1) * SUB, :] = low[:, t * HD : (t + 1) * HD].astype(BF)
    tail = tail_of(rest)
    both = tail[: SUB // 2] + pltpu.roll(tail[SUB // 2 :], HD // 2, 1)
    ref[k, TILES * SUB : BLOCK, :] = both.astype(BF)


def rest_of(both):
    return whole_tail(jnp.concatenate([both, pltpu.roll(both, HD // 2, 1)], axis=0))


def fetch(pairs, sems):
    copies = [pltpu.make_async_copy(a, b, sems.at[i]) for i, (a, b) in enumerate(pairs)]
    for copy in copies:
        copy.start()
    return copies


def pack_kernel(entries_hbm, q_hbm, cache_hbm, out_ref, tab, entries, q_ref, cache_ref, sems):
    copies = fetch([(entries_hbm, entries), (q_hbm, q_ref), (cache_hbm, cache_ref)], sems)
    me = lax.axis_index("req")
    for i in range(TABLE):
        tab[i] = 0
    copies[0].wait()
    for i in range(REQ):
        owner = entries[me * REQ + i] >> SHIFT
        count = tab[5 * REQ + owner]
        tab[jnp.minimum(count, 1) * REQ + owner] = i
        tab[5 * REQ + owner] = count + 1

    def one_peer(p, carry):
        first, last = jnp.int32(REQ - 1), jnp.int32(-1)
        for i in range(REQ):
            match = entries[p * REQ + i] >> SHIFT == me
            first = jnp.minimum(first, jnp.where(match, i, REQ - 1))
            last = jnp.where(match, i, last)
        tab[2 * REQ + p] = first
        tab[3 * REQ + p] = jnp.maximum(last, 0)
        tab[4 * REQ + p] = (last >= 0).astype(jnp.int32)
        return carry

    lax.fori_loop(0, REQ, one_peer, 0, unroll=2)
    copies[1].wait()
    copies[2].wait()
    for p in range(REQ):
        for k in range(2):
            slot = tab[k * REQ + p]
            out_ref[p, k * NEW : (k + 1) * NEW, :] = q_ref[
                pl.ds(pl.multiple_of(slot * NEW, NEW), NEW), :
            ]
            entry = entries[p * REQ + tab[(2 + k) * REQ + p]] & (REQ - 1)
            out_ref[p, 2 * NEW + k * NS : 2 * NEW + (k + 1) * NS, :] = cache_ref[entry].astype(BF)


def project_kernel(x_ref, w_ref, after, own_ref, far_ref, sent):
    at = lax.axis_index("mp")
    member = (at // (lax.axis_size("mp") // 2)) * 2 + (at & 1)
    for d in range(4):
        first = pl.multiple_of((member ^ d) * CHUNK, CHUNK)
        rows = x_ref[pl.ds(first, CHUNK), :]
        low = jnp.dot(rows, w_ref[:, :RANK], preferred_element_type=F32)
        rest = jnp.dot(rows, w_ref[:, RANK:], preferred_element_type=F32)
        rest = jnp.concatenate([rest, jnp.zeros((CHUNK, COLS - RANK - BC), F32)], axis=1)
        if d % 2 == 0:
            kept = far_ref if d else own_ref
            kept[:, :RANK] = low
            kept[:, RANK:] = rest
        else:
            for k in range(CHUNK // SUB):
                some = slice(k * SUB, (k + 1) * SUB)
                store_block(sent, d // 2 * (CHUNK // SUB) + k, low[some], rest[some])


def add_block(kept, k, block, out_ref):
    some = slice(k * SUB, (k + 1) * SUB)
    tiles = [block[t * SUB : (t + 1) * SUB] for t in range(TILES)]
    low = kept[some, :RANK] + jnp.concatenate(tiles, axis=1)
    store_block(out_ref, k, low, kept[some, RANK:] + rest_of(block[TILES * SUB :]))


def add_two_kernel(far_ref, r1, after, out_ref):
    for k in range(CHUNK // SUB):
        add_block(far_ref, k, r1[CHUNK // SUB + k].astype(F32), out_ref)


def add_four_kernel(own_ref, r1, r2, out_ref):
    for k in range(CHUNK // SUB):
        add_block(own_ref, k, r1[k].astype(F32) + r2[k].astype(F32), out_ref)


def add_eight_kernel(parts, after, out_ref):
    block = parts[0].astype(F32)
    for k in range(1, CHUNK // SUB):
        block = block + parts[k].astype(F32)
    low = jnp.concatenate([block[t * SUB : (t + 1) * SUB] for t in range(TILES)], axis=1)
    rest = rest_of(block[TILES * SUB :])
    for k in range(CHUNK // SUB):
        store_block(out_ref, k, low, rest)


def gate_kernel(partial, after, out):
    pass


def heads_down(block):
    return jnp.concatenate([block[:, :HD], block[:, HD:]], axis=0)


def cached_kernel(tab, table, kept, got_ref, pool_ref, out_ref, done_ref):
    done_ref[...] = jnp.zeros(done_ref.shape, F32)
    row = lax.broadcasted_iota(jnp.int32, (2 * NEW, HD), 0)
    lane = lax.broadcasted_iota(jnp.int32, (2 * NEW, HD), 1)
    key = lax.broadcasted_iota(jnp.int32, (2 * NEW, KEEP), 1)
    base = lax.axis_index("req") * (REQ * PAGES)

    def one_peer(p, carry):
        @pl.when(tab[4 * REQ + p] > 0)
        def _():
            stats = []
            for k in range(2):
                slot = p * REQ + tab[(2 + k) * REQ + p]
                pages = [pool_ref[table[t * REQ * REQ + slot] - base] for t in range(PAGES)]
                rows = jnp.concatenate(pages, axis=0)
                q = heads_down(got_ref[p, k * NEW : (k + 1) * NEW, :])
                s = lax.dot_general(
                    q, rows[:, :HD], (((1,), (1,)), ((), ())), preferred_element_type=F32
                ) * (HD**-0.5)
                s = jnp.where(key < kept[slot], s, -1e30)
                top = jnp.max(s, axis=1, keepdims=True)
                w = jnp.exp(s - top)
                total = jnp.sum(w, axis=1, keepdims=True)
                o = jnp.dot(w.astype(BF), rows[:, HD:], preferred_element_type=F32) / total
                out_ref[p, k * NEW : (k + 1) * NEW, :] = jnp.concatenate(
                    [o[:NEW], o[NEW:]], axis=1
                ).astype(BF)
                lse = top + jnp.log(total)
                stats.append(jnp.sum(jnp.where(row == lane, lse, 0.0), axis=0, keepdims=True))
            flat = jnp.concatenate(stats, axis=0)
            hi = flat.astype(BF).astype(F32)
            mid = (flat - hi).astype(BF).astype(F32)
            low = flat - hi - mid
            none = jnp.zeros((6, HD), F32)
            left = jnp.concatenate([hi, low, none[:4]], axis=0)
            right = jnp.concatenate([mid, none], axis=0)
            out_ref[p, STAT:RET, :] = jnp.concatenate([left, right], axis=1).astype(BF)

        return carry

    lax.fori_loop(0, REQ, one_peer, 0)


def fresh_kernel(q_ref, kv_ref, out_ref, stat_ref):
    row = lax.broadcasted_iota(jnp.int32, (2 * NEW, HD), 0)
    lane = lax.broadcasted_iota(jnp.int32, (2 * NEW, HD), 1)
    query = lax.broadcasted_iota(jnp.int32, (2 * NEW, NEW), 0) & (NEW - 1)
    key = lax.broadcasted_iota(jnp.int32, (2 * NEW, NEW), 1)

    def one_slot(i, carry):
        first = pl.multiple_of(i * NEW, NEW)
        q = heads_down(q_ref[pl.ds(first, NEW), :])
        rows = kv_ref[pl.ds(first, NEW), :]
        s = lax.dot_general(
            q, rows[:, :HD], (((1,), (1,)), ((), ())), preferred_element_type=F32
        ) * (HD**-0.5)
        s = jnp.where(key <= query, s, -1e30)
        top = jnp.max(s, axis=1, keepdims=True)
        w = jnp.exp(s - top)
        total = jnp.sum(w, axis=1, keepdims=True)
        out_ref[i] = jnp.dot(w.astype(BF), rows[:, HD:], preferred_element_type=F32) / total
        lse = top + jnp.log(total)
        flat = jnp.sum(jnp.where(row == lane, lse, 0.0), axis=0, keepdims=True)
        stat_ref[i] = jnp.broadcast_to(flat, (8, HD))
        return carry

    lax.fori_loop(0, REQ, one_slot, 0, unroll=4)


def combine_kernel(tab, entries, fresh_len, part_ref, stat_ref, got_ref, after, out_ref):
    base = lax.axis_index("req") * REQ
    row = lax.broadcasted_iota(jnp.int32, (2 * NEW, HD), 0)
    lane = lax.broadcasted_iota(jnp.int32, (2 * NEW, HD), 1)
    spot = lax.broadcasted_iota(jnp.int32, (NEW, 2 * HD), 0)

    def one_slot(i, carry):
        first = pl.multiple_of(i * NEW, NEW)
        owner = entries[base + i] >> SHIFT
        second = (tab[REQ + owner] == i).astype(jnp.int32)
        old = heads_down(
            got_ref[owner, pl.ds(pl.multiple_of(second * NEW, NEW), NEW), :]
        ).astype(F32)
        stats = got_ref[owner, STAT:RET, :].astype(F32)
        exact = stats[0:2, :HD] + stats[0:2, HD:] + stats[2:4, :HD]
        lse_old = jnp.where(second > 0, exact[1:2], exact[0:1])
        lse = stat_ref[i, 0:1, :]
        most = jnp.maximum(lse_old, lse)
        weight_old = jnp.exp(lse_old - most)
        weight = jnp.exp(lse - most)
        share_old = weight_old / (weight_old + weight)
        share_old = jnp.sum(jnp.where(row == lane, share_old, 0.0), axis=1, keepdims=True)
        share = weight / (weight_old + weight)
        share = jnp.sum(jnp.where(row == lane, share, 0.0), axis=1, keepdims=True)
        o = old * share_old + part_ref[i] * share
        o = jnp.concatenate([o[:NEW], o[NEW:]], axis=1)
        live = spot < fresh_len[base + i]
        out_ref[pl.ds(first, NEW), :] = jnp.where(live, o, 0.0).astype(BF)
        return carry

    lax.fori_loop(0, REQ, one_slot, 0, unroll=4)


def scan_kernel(
    tab, entries, fresh_len, low_ref, wdt_hbm, b_ref, a_ref, d_ref, x_hbm, g_hbm, got_hbm,
    out_ref, state_ref, done_ref, dt_s, u_s, bc_s, y_s, a_s, h_s, wdt_ref, x_ref, g_ref, got_ref, sems,
):
    copies = fetch(
        [(wdt_hbm, wdt_ref), (x_hbm, x_ref), (got_hbm, got_ref), (g_hbm, g_ref)], sems
    )
    done_ref[...] = jnp.zeros(done_ref.shape, F32)
    base = lax.axis_index("req") * REQ
    channels = x_ref.shape[1]
    halves = [slice(c * HD, (c + 1) * HD) for c in range(channels // HD)]
    step = lax.broadcasted_iota(jnp.int32, (NEW, channels), 0)
    for n in range(NS):
        a_s[n * 8 : (n + 1) * 8, :] = jnp.broadcast_to(a_ref[n : n + 1, :] * (-LOG2E), (8, channels))
    for at in range(low_ref.shape[0]):
        bc_s[at * SUB : (at + 1) * SUB, :] = rest_of(low_ref[at, TILES * SUB : BLOCK, :].astype(F32))
    copies[0].wait()
    copies[1].wait()
    for member in range(4):
        first = member * CHUNK
        low = []
        for k in range(CHUNK // SUB):
            at = member * (CHUNK // SUB) + k
            tiles = [low_ref[at, t * SUB : (t + 1) * SUB, :] for t in range(TILES)]
            low.append(jnp.concatenate(tiles, axis=1))
        low = jnp.concatenate(low, axis=0)
        pre = jnp.dot(low, wdt_ref[...], preferred_element_type=F32) + b_ref[...]
        dt = jnp.maximum(pre, 0.0) + jnp.log1p(jnp.exp(-jnp.abs(pre)))
        for j in range(CHUNK // NEW):
            here = first + j * NEW
            live = step < fresh_len[base + member * (CHUNK // NEW) + j]
            masked = jnp.where(live, dt[j * NEW : (j + 1) * NEW], 0.0)
            drive = masked * x_ref[pl.ds(here, NEW), :].astype(F32)
            for c, half in enumerate(halves):
                dt_s[c, pl.ds(here, NEW), :] = masked[:, half]
                u_s[c, pl.ds(here, NEW), :] = drive[:, half]
    copies[2].wait()
    for i in range(REQ):
        owner = entries[base + i] >> SHIFT
        second = (tab[REQ + owner] == i).astype(jnp.int32)
        start = pl.multiple_of(2 * NEW + second * NS, NS)
        state = got_ref[owner, pl.ds(start, NS), :].astype(F32)
        for c, half in enumerate(halves):
            h_s[c, i * NS : (i + 1) * NS, :] = state[:, half]
    for g in range(2):
        begin = g * 8 * NS
        h0 = tuple(
            tuple(h_s[c, pl.ds(begin + n, 8, stride=NS), :] for c in range(len(halves)))
            for n in range(NS)
        )

        def one_step(i, hs):
            rows = pl.ds(g * 8 * NEW + i, 8, stride=NEW)
            dt = [dt_s[c, rows, :] for c in range(len(halves))]
            u = [u_s[c, rows, :] for c in range(len(halves))]
            bc = bc_s[rows, :]
            y = [0.0] * len(halves)
            new = []
            for n in range(NS):
                b_in = jnp.broadcast_to(bc[:, n : n + 1], (8, HD))
                c_out = jnp.broadcast_to(bc[:, NS + n : NS + n + 1], (8, HD))
                pair = []
                for c, half in enumerate(halves):
                    decay = jnp.exp2(dt[c] * a_s[n * 8 : (n + 1) * 8, half])
                    h = decay * hs[n][c] + u[c] * b_in
                    y[c] = y[c] + h * c_out
                    pair.append(h)
                new.append(tuple(pair))
            for c in range(len(halves)):
                y_s[c, rows, :] = y[c]
            return tuple(new)

        hs = lax.fori_loop(0, NEW, one_step, h0, unroll=16)
        for n in range(NS):
            for c in range(len(halves)):
                h_s[c, pl.ds(begin + n, 8, stride=NS), :] = hs[n][c]
    for c, half in enumerate(halves):
        state_ref[:, half] = h_s[c]
    copies[3].wait()
    for i in range(REQ):
        rows = slice(i * NEW, (i + 1) * NEW)
        for c, half in enumerate(halves):
            gate = g_ref[rows, half].astype(F32)
            y = y_s[c, rows, :] + d_ref[:, half] * x_ref[rows, half].astype(F32)
            y = y * (gate * jax.nn.sigmoid(gate))
            out_ref[rows, half] = jnp.where(step[:, half] < fresh_len[base + i], y, 0.0).astype(BF)


def on_device(
    queries, kv_new, kv_pool, ssm_cache, mixer_in, gate_in, w_x, w_dt, b_dt, a_rate, d_skip,
    kept_len, new_len, cache_index, page_table,
):
    rows, channels = mixer_in.shape
    zs = lax.axis_size("mp") // 2

    packed, tab = pl.pallas_call(
        pack_kernel,
        out_shape=[
            jax.ShapeDtypeStruct((REQ, SEND, channels), BF),
            jax.ShapeDtypeStruct((TABLE,), jnp.int32),
        ],
        in_specs=[HBM, HBM, HBM],
        out_specs=[VMEM, SMEM],
        scratch_shapes=[
            pltpu.SMEM(cache_index.shape, jnp.int32),
            pltpu.VMEM(queries.shape, BF),
            pltpu.VMEM(ssm_cache.shape, F32),
            pltpu.SemaphoreType.DMA((3,)),
        ],
        compiler_params=PARAMS,
        name="pack",
    )(cache_index, queries, ssm_cache)
    got = lax.all_to_all(packed, "req", 0, 0, tiled=True)

    chunk = jax.ShapeDtypeStruct((CHUNK // SUB, BLOCK, HD), BF)
    own, far, sent = pl.pallas_call(
        project_kernel,
        out_shape=[
            jax.ShapeDtypeStruct((CHUNK, COLS), F32),
            jax.ShapeDtypeStruct((CHUNK, COLS), F32),
            jax.ShapeDtypeStruct((2 * CHUNK // SUB, BLOCK, HD), BF),
        ],
        in_specs=[VMEM, VMEM, ANY],
        out_specs=[VMEM] * 3,
        compiler_params=SMALL,
        name="project",
    )(mixer_in, w_x, packed)

    def swap(array, d):
        pairs = []
        for i in range(2 * zs):
            y, z = i // zs, i % zs
            pairs.append((i, (y ^ (d >> 1)) * zs + (z ^ (d & 1))))
        return lax.ppermute(array, "mp", pairs)

    quads = [[y * zs + 2 * k + b for y in range(2) for b in range(2)] for k in range(zs // 2)]
    groups = [[y * zs + 2 * k + b for k in range(zs // 2)] for y in range(2) for b in range(2)]
    block = jax.ShapeDtypeStruct((REQ, 2 * NEW, HD), F32)
    fresh = pl.pallas_call(
        fresh_kernel,
        out_shape=[block, jax.ShapeDtypeStruct((REQ, 8, HD), F32)],
        in_specs=[VMEM] * 2,
        out_specs=[VMEM] * 2,
        compiler_params=SMALL,
        name="fresh",
    )(queries, kv_new.reshape(rows, channels))
    near = swap(sent, 1)
    pair = pl.pallas_call(
        add_two_kernel,
        out_shape=chunk,
        in_specs=[VMEM] * 2 + [ANY],
        out_specs=VMEM,
        compiler_params=SMALL,
        name="add_two",
    )(far, near, fresh[1])
    across = swap(pair, 2)
    added = pl.pallas_call(
        add_four_kernel,
        out_shape=chunk,
        in_specs=[VMEM] * 3,
        out_specs=VMEM,
        compiler_params=SMALL,
        name="add_four",
    )(own, near, across)
    token = jax.ShapeDtypeStruct((8, HD), F32)
    partial, cached = pl.pallas_call(
        cached_kernel,
        out_shape=[jax.ShapeDtypeStruct((REQ, RET, channels), BF), token],
        in_specs=[SMEM, SMEM, SMEM, VMEM, VMEM],
        out_specs=[VMEM] * 2,
        compiler_params=SMALL,
        name="cached",
    )(tab, page_table.T.reshape(-1), kept_len, got, kv_pool.reshape(-1, PAGE, channels))
    parts = lax.all_to_all(added, "mp", 0, 0, tiled=True, axis_index_groups=groups)
    summed = pl.pallas_call(
        add_eight_kernel,
        out_shape=chunk,
        in_specs=[VMEM, ANY],
        out_specs=VMEM,
        compiler_params=SMALL,
        name="add_eight",
    )(parts, cached)
    whole = lax.all_to_all(summed, "mp", 0, 0, tiled=True, axis_index_groups=groups)
    whole = jnp.concatenate([whole] * 4, axis=0)
    whole = lax.all_to_all(whole, "mp", 0, 0, tiled=True, axis_index_groups=quads)

    partial = pl.pallas_call(
        gate_kernel,
        out_shape=jax.ShapeDtypeStruct(partial.shape, BF),
        in_specs=[ANY] * 2,
        out_specs=ANY,
        input_output_aliases={0: 0},
        compiler_params=PARAMS,
        name="gate",
    )(partial, whole)
    back = lax.all_to_all(partial, "req", 0, 0, tiled=True)

    mixer_out, state_out, done = pl.pallas_call(
        scan_kernel,
        out_shape=[
            jax.ShapeDtypeStruct((rows, channels), BF),
            jax.ShapeDtypeStruct((REQ * NS, channels), F32),
            token,
        ],
        in_specs=[SMEM] * 3 + [VMEM, HBM] + [VMEM] * 3 + [HBM] * 3,
        out_specs=[VMEM] * 3,
        scratch_shapes=[
            pltpu.VMEM((channels // HD, rows, HD), F32),
            pltpu.VMEM((channels // HD, rows, HD), F32),
            pltpu.VMEM((rows, COLS - RANK), F32),
            pltpu.VMEM((channels // HD, rows, HD), F32),
            pltpu.VMEM((NS * 8, channels), F32),
            pltpu.VMEM((channels // HD, REQ * NS, HD), F32),
            pltpu.VMEM(w_dt.shape, BF),
            pltpu.VMEM((rows, channels), BF),
            pltpu.VMEM((rows, channels), BF),
            pltpu.VMEM(got.shape, BF),
            pltpu.SemaphoreType.DMA((4,)),
        ],
        compiler_params=MIDDLE,
        name="scan",
    )(
        tab, cache_index, new_len, whole, w_dt, b_dt.reshape(1, -1), a_rate,
        d_skip.reshape(1, -1), mixer_in, gate_in, got,
    )
    attn_out = pl.pallas_call(
        combine_kernel,
        out_shape=jax.ShapeDtypeStruct((rows, channels), BF),
        in_specs=[SMEM] * 3 + [VMEM] * 3 + [ANY],
        out_specs=VMEM,
        compiler_params=SMALL,
        name="combine",
    )(tab, cache_index, new_len, *fresh, back, done)
    return attn_out, mixer_out, state_out.reshape(REQ, NS, channels)


def solution(mesh):
    placed = (
        P("req", "mp"),
        P("req", "mp", None),
        P("req", None, "mp", None),
        P("req", None, "mp"),
        P("req", "mp"),
        P("req", "mp"),
        P("mp", None),
        P(None, "mp"),
        P("mp"),
        P(None, "mp"),
        P("mp"),
        P(),
        P(),
        P(),
        P(),
    )
    return jax.shard_map(
        on_device,
        mesh=mesh,
        in_specs=placed,
        out_specs=(P("req", "mp"), P("req", "mp"), P("req", None, "mp")),
        check_vma=False,
    )
```
